512 devices in a mesh: level: 8 (over z_lo), row: 8 (over x, z_hi), col: 8 (over y, core).
Axes of the slice: x: 4, y: 4, z: 16 (z_hi: 2, z_lo: 8; z = z_hi * 8 + z_lo), core: 2. Of those that a mesh axis runs over, the one named last changes fastest.
Arguments:
- leaf_blocks: bfloat16 [8, 24576, 2048], P('level', 'row', 'col'), may hold values from -3 to 3
- leaf_tiles: int32 [8], replicated, may hold values from 64 to 96, as said below
- leaf_maps: int32 [8, 96], replicated, may hold values from 0 to 127, as said below
- upper_maps: int32 [4, 128], replicated, may hold values from 0 to 127, as said below
- front_slots: int32 [6, 8], replicated, may hold values from 0 to 7, as said below
- pivot_diag: float32 [6, 256], replicated, may hold values from 96 to 192
Outputs:
- top_blocks: bfloat16 [8, 8192, 2048], P('level', 'row', 'col')
The draws below stay inside these ranges and needn't reach their ends.
Inputs may be any that keep to these rules, and one draw needn't show every extreme that they name: `leaf_tiles`: each sibling pair 2i, 2i + 1 holds one block of exactly 96 tiles and one of fewer; some pair holds one of 64 tiles. `leaf_maps`: each row sends distinct leaf tiles to distinct front tiles. Cut the leaf tiles into aligned blocks of 12 and the front tiles into aligned blocks of 8; front block k belongs to row group k mod 8. From one leaf block exactly 2 tiles go to the blocks of each of four row groups and exactly 1 tile to each of the other four. `upper_maps`: each row is a permutation of the 128 tiles. Cut a lower front into aligned blocks of 8 tiles and the upper front into aligned blocks of 4; upper block k belongs to row group k mod 8. From one lower block exactly 1 tile goes to the blocks of each row group. `front_slots`: each row is a permutation of the window positions. The slot at position 0 of an upper front is at position 0 in neither of its two children.
All inputs are finite; a program needn't handle non-finite values.
Results may differ from the reference program's by a relative error of at most 0.009.
Values may be sent and summed in bfloat16 or wider, within the bound.
No kernel may reach another device: no remote copies, remote signals or barrier semaphores. Data moves between devices by JAX's collectives and lax.ppermute only.
A program may use at most 64 MiB of HBM per device.

```python
import math
import jax
import jax.numpy as jnp
from jax import lax

TILE = 256
NP = 32768
NPT = 128
CBT = 96
LEAVES = 8
FRONTS = 6
WINDOW = 8
LEAF_BLOCK = 12
LOWER_BLOCK = 8
N_ROW = 8


def shuffle_rows(key, row_total, length):
    row_keys = jax.random.split(key, row_total)
    return jax.vmap(lambda row_key: jax.random.permutation(row_key, length))(row_keys)


def tile_map(key, block_count, block_tiles, cube_count):
    tile_count = block_count * block_tiles
    front_local = NPT // (cube_count * N_ROW)
    order_key, row_key, cube_key, slot_key = jax.random.split(key, 4)
    within = shuffle_rows(order_key, block_count, block_tiles)
    block_ids = jnp.arange(block_count)[:, None]
    row_perm = jax.random.permutation(row_key, N_ROW)
    dest_rows = row_perm[(within + block_ids) % N_ROW].reshape(-1)
    positions = jnp.arange(tile_count)
    earlier = positions[None, :] < positions[:, None]
    same_row = dest_rows[:, None] == dest_rows[None, :]
    row_rank = jnp.sum(jnp.logical_and(same_row, earlier), axis=1)
    cube_perm = jax.random.permutation(cube_key, cube_count)
    cube_pos = cube_perm[row_rank % cube_count]
    dest_dev = cube_pos * N_ROW + dest_rows
    slot_perm = shuffle_rows(slot_key, cube_count * N_ROW, front_local)
    local_slot = slot_perm[dest_dev, row_rank // cube_count]
    return (dest_dev * front_local + local_slot).astype(jnp.int32)


def draw_leaf_blocks(key, part):
    key = jax.random.fold_in(key, 11)
    full_shape = (LEAVES, CBT * TILE, WINDOW * TILE)
    return jax.random.uniform(key, full_shape, jnp.float32, -3.0, 3.0).astype(jnp.bfloat16)


def draw_leaf_tiles(key, part):
    key = jax.random.fold_in(key, 3)
    flip_key, size_key, pick_key = jax.random.split(key, 3)
    pair_count = LEAVES // 2
    flip_bits = jax.random.randint(flip_key, (pair_count,), 0, 2)
    smallest = CBT - CBT // 3
    smaller = jax.random.randint(size_key, (pair_count,), smallest, CBT)
    forced = jax.random.randint(pick_key, (), 0, pair_count)
    smaller = jnp.where(jnp.arange(pair_count) == forced, smallest, smaller)
    first_size = jnp.where(flip_bits == 1, smaller, CBT)
    second_size = jnp.where(flip_bits == 1, CBT, smaller)
    return jnp.stack([first_size, second_size], axis=1).reshape(LEAVES).astype(jnp.int32)


def draw_leaf_maps(key, part):
    key = jax.random.fold_in(key, 5)
    leaf_keys = jax.random.split(key, LEAVES)
    return jax.vmap(lambda leaf_key: tile_map(leaf_key, N_ROW, LEAF_BLOCK, 2))(leaf_keys)


def draw_upper_maps(key, part):
    key = jax.random.fold_in(key, 7)
    front_keys = jax.random.split(key, LEAVES // 2)
    return jax.vmap(lambda front_key: tile_map(front_key, 2 * N_ROW, LOWER_BLOCK, 4))(front_keys)


def draw_front_slots(key, part):
    key = jax.random.fold_in(key, 9)
    lower_key, score_key, rest_key = jax.random.split(key, 3)
    lower_places = shuffle_rows(lower_key, LEAVES // 2, WINDOW)
    positions = jnp.arange(WINDOW)
    pivots = jnp.sum(jnp.where(lower_places == 0, positions[None, :], 0), axis=1)
    blocked = jnp.logical_or(positions[None, :] == pivots[0::2, None], positions[None, :] == pivots[1::2, None])
    scores = jax.random.randint(score_key, (LEAVES // 4, WINDOW), 0, 1 << 20) + jnp.where(blocked, 1 << 21, 0)
    chosen = jnp.argmin(scores, axis=1)
    rest_places = shuffle_rows(rest_key, LEAVES // 4, WINDOW - 1) + 1
    rest_index = jnp.clip(positions[None, :] - (positions[None, :] > chosen[:, None]).astype(jnp.int32), 0, WINDOW - 2)
    upper_places = jnp.where(positions[None, :] == chosen[:, None], 0, jnp.take_along_axis(rest_places, rest_index, axis=1))
    return jnp.concatenate([lower_places, upper_places], axis=0).astype(jnp.int32)


def setup_inputs(seed: int = 0) -> dict:
    key_list = jax.random.split(jax.random.key(seed), 7)
    leaf_blocks = draw_leaf_blocks(jax.random.fold_in(key_list[6], 71), 0)
    leaf_tiles = draw_leaf_tiles(jax.random.fold_in(key_list[6], 71), 0)
    leaf_maps = draw_leaf_maps(jax.random.fold_in(key_list[6], 71), 0)
    upper_maps = draw_upper_maps(jax.random.fold_in(key_list[6], 71), 0)
    front_slots = draw_front_slots(jax.random.fold_in(key_list[6], 71), 0)
    pivot_diag = jnp.clip(jnp.exp(jax.random.uniform(key_list[5], (FRONTS, TILE), jnp.float32, math.log(96.0), math.log(192.0))), 96.0, 192.0)
    return dict(leaf_blocks=leaf_blocks, leaf_tiles=leaf_tiles, leaf_maps=leaf_maps, upper_maps=upper_maps, front_slots=front_slots, pivot_diag=pivot_diag)


def masked_leaf(leaf_blocks, leaf_tiles, leaf_index):
    row_index = jnp.arange(CBT * TILE, dtype=jnp.int32)
    keep_rows = row_index < leaf_tiles[leaf_index] * TILE
    return jnp.where(keep_rows[:, None], leaf_blocks[leaf_index], jnp.zeros((), jnp.bfloat16))

def merge_front(first_block, second, first_map, second_map, slot_place, diagonal):
    slot_count = slot_place.shape[0]
    columns = slot_count * TILE
    zero_front = jnp.zeros((NPT, TILE, columns), jnp.bfloat16)
    placed_first = zero_front.at[first_map].set(first_block.reshape(-1, TILE, columns))
    placed_second = zero_front.at[second_map].set(second.reshape(-1, TILE, columns))
    assembled = placed_first.astype(jnp.float32) + placed_second.astype(jnp.float32)
    positions = jnp.arange(slot_count, dtype=jnp.int32)
    pivot_slot = jnp.sum(jnp.where(slot_place == 0, positions, 0)).astype(jnp.int32)
    column = lax.dynamic_slice_in_dim(assembled, pivot_slot * TILE, TILE, 2)
    corner = column[0]
    corner = (corner + corner.T) * 0.5 + jnp.diag(diagonal)
    factor = jnp.linalg.cholesky(corner)
    column = column.at[0].set(corner)
    panel_rows = lax.linalg.triangular_solve(factor, column.reshape(NP, TILE), left_side=False, lower=True, transpose_a=True)
    panel_rows = panel_rows.astype(jnp.bfloat16)
    chosen = panel_rows.reshape(NPT, TILE, TILE)[slot_place * (NPT // slot_count)]
    update = jnp.einsum('ik,cjk->icj', panel_rows.astype(jnp.float32), chosen.astype(jnp.float32), precision=lax.Precision.HIGHEST)
    result = assembled.reshape(NP, slot_count, TILE) - update
    keep_rows = jnp.arange(NP, dtype=jnp.int32) >= TILE
    keep_cols = positions != pivot_slot
    keep_mask = jnp.logical_and(keep_rows[:, None, None], keep_cols[None, :, None])
    result = jnp.where(keep_mask, result, jnp.zeros((), jnp.float32))
    return result.reshape(NP, columns).astype(jnp.bfloat16)

def reference(leaf_blocks, leaf_tiles, leaf_maps, upper_maps, front_slots, pivot_diag):
    lower_fronts = []
    for front_index in range(LEAVES // 2):
        first_leaf = 2 * front_index
        second_leaf = 2 * front_index + 1
        lower_fronts.append(merge_front(masked_leaf(leaf_blocks, leaf_tiles, first_leaf), masked_leaf(leaf_blocks, leaf_tiles, second_leaf), leaf_maps[first_leaf], leaf_maps[second_leaf], front_slots[front_index], pivot_diag[front_index]))
    upper_fronts = []
    for front_index in range(LEAVES // 4):
        upper_fronts.append(merge_front(lower_fronts[2 * front_index], lower_fronts[2 * front_index + 1], upper_maps[2 * front_index], upper_maps[2 * front_index + 1], front_slots[LEAVES // 2 + front_index], pivot_diag[LEAVES // 2 + front_index]))
    quarters = []
    for leaf_index in range(LEAVES):
        whole_front = upper_fronts[leaf_index // 4]
        quarters.append(whole_front.reshape(4, NP // 4, whole_front.shape[1])[leaf_index % 4])
    return jnp.stack(quarters)
```

```python
import functools

import jax
import jax.numpy as jnp
from jax import lax
from jax.experimental import pallas as pl
from jax.experimental.pallas import tpu as pltpu
from jax.sharding import PartitionSpec as P

TILE = 256
NPT = 128
STEP = 32
GROUP = 128
HIGHEST = lax.Precision.HIGHEST
VMEM = pltpu.VMEM
SMEM = pltpu.SMEM
INTERPRET = False
F32 = jnp.float32
BF16 = jnp.bfloat16


def call(kernel, out_shape, in_spaces, out_space=None, scratch=(), flops=0, moved=0):
    return pl.pallas_call(
        kernel,
        out_shape=out_shape,
        in_specs=[pl.BlockSpec(memory_space=space) for space in in_spaces],
        out_specs=pl.BlockSpec(memory_space=out_space)
        if out_space is not None
        else [pl.BlockSpec(memory_space=VMEM) for _ in out_shape],
        scratch_shapes=list(scratch),
        compiler_params=pltpu.CompilerParams(vmem_limit_bytes=32 * 2**20),
        cost_estimate=pl.CostEstimate(flops=flops, bytes_accessed=moved, transcendentals=0),
        interpret=INTERPRET,
    )


def plan_kernel(meta_ref, tiles_ref, leaf_maps_ref, upper_maps_ref, place_ref):
    level, row = meta_ref[0], meta_ref[1]
    half = row % 2
    base = level // 4 * 4

    def one(index, carry):
        source, tile = index // 12, index % 12
        quad, across = source // 4, source % 4
        leaf = base + quad
        leaf_tile = (2 * across + half) * 12 + tile
        lower_tile = leaf_maps_ref[leaf, leaf_tile]
        upper_tile = upper_maps_ref[leaf // 2, lower_tile]
        kept = jnp.logical_and(leaf_tile < tiles_ref[leaf], lower_tile != 0)
        home_row = upper_tile // 4 % 8
        position = (upper_tile // 32 * 4 + home_row // 2) * 4 + upper_tile % 4
        other = (home_row % 2 != half).astype(jnp.int32)
        place_ref[index] = jnp.where(kept, position + 64 * other, 128)
        return carry

    lax.fori_loop(0, 192, one, 0)


def pick_kernel(meta_ref, tiles_ref, leaf_maps_ref, slots_ref, pivot_ref, out_ref):
    level, row, col = meta_ref[0], meta_ref[1], meta_ref[2]
    tile = pivot_ref.shape[1]
    wanted = (0, slots_ref[level // 2, col] * 16)
    parts, across, rows = out_ref.shape[1], out_ref.shape[0], out_ref.shape[2]
    for part in range(parts):

        def look(index, found):
            leaf_tile = row * 12 + index
            match = jnp.logical_and(
                leaf_maps_ref[level, leaf_tile] == wanted[part], leaf_tile < tiles_ref[level]
            )
            return jnp.where(match, index, found)

        found = lax.fori_loop(0, 12, look, jnp.int32(-1))
        value = pivot_ref[jnp.maximum(found, 0)]
        value = jnp.where(found >= 0, value, jnp.zeros_like(value))
        out_ref[:, part] = value.reshape(across, rows, tile)


def eliminate(pivot, panel_tile, diagonal, work_ref):
    tile = pivot.shape[0]
    width = 2 * tile
    rows = lax.broadcasted_iota(jnp.int32, (tile, tile), 0)
    columns = lax.broadcasted_iota(jnp.int32, (tile, tile), 1)
    work_ref[:, :tile] = (pivot + pivot.T) * 0.5 + jnp.where(rows == columns, diagonal, 0.0)
    work_ref[:, tile:] = panel_tile.T
    group = min(GROUP, tile)
    for start in range(0, tile, STEP):
        low = start // group * group
        offset = start - low
        block = work_ref[start : start + STEP, low:]
        row_ids = lax.broadcasted_iota(jnp.int32, block.shape, 0)
        for step in range(STEP):
            lane = offset + step
            column = block[:, lane : lane + 1]
            pivot_row = block[step : step + 1, :] * (1.0 / block[step : step + 1, lane : lane + 1])
            block = jnp.where(row_ids == step, pivot_row, block - column * pivot_row)
        work_ref[start : start + STEP, low:] = block
        factor = work_ref[:, low : low + group]
        fac_rows = lax.broadcasted_iota(jnp.int32, factor.shape, 0)
        fac_cols = lax.broadcasted_iota(jnp.int32, factor.shape, 1)
        own_row = jnp.logical_and(fac_rows >= start, fac_rows < start + STEP)
        own_col = jnp.logical_and(fac_cols >= offset, fac_cols < offset + STEP)
        factor = jnp.where(jnp.logical_and(own_col, jnp.logical_not(own_row)), factor, 0.0)
        pieces = [block]
        if offset:
            pieces.insert(0, jnp.zeros((offset, width - low), F32))
        if group - offset - STEP:
            pieces.append(jnp.zeros((group - offset - STEP, width - low), F32))
        spread = jnp.concatenate(pieces, axis=0) if len(pieces) > 1 else block
        work_ref[:, low:] = work_ref[:, low:] - jnp.dot(
            factor, spread, precision=HIGHEST, preferred_element_type=F32
        )
    return work_ref[:, tile:]


def pivot_slot_of(slots_ref, front):
    slot = jnp.int32(0)
    for index in range(8):
        slot = jnp.where(slots_ref[front, index] == 0, index, slot)
    return slot


def lower_kernel(meta_ref, slots_ref, diag_ref, gathered_ref, leaf_ref, pivot_ref, out_ref, work_ref):
    level, col = meta_ref[0], meta_ref[2]
    tile = leaf_ref.shape[1]
    pivot = gathered_ref[:, 0].reshape(tile, tile).astype(F32)
    chosen = gathered_ref[:, 1].reshape(tile, tile).astype(F32)
    front = level // 2
    solved = eliminate(pivot, chosen, diag_ref[pl.ds(front, 1), :], work_ref).astype(BF16)
    dropped = pivot_slot_of(slots_ref, front) == col

    def one(index, carry):
        update = jnp.dot(pivot_ref[index], solved, preferred_element_type=F32)
        result = leaf_ref[index].astype(F32) - update
        result = jnp.where(dropped, 0.0, result).astype(BF16)
        out_ref[:, index] = result.reshape(out_ref.shape[0], out_ref.shape[2], tile)
        return carry

    lax.fori_loop(0, 12, one, 0)


def sum_kernel(place_ref, chunks_ref, keep_ref, send_ref, total_ref):
    total_ref[...] = jnp.zeros_like(total_ref)

    def one(index, carry):
        place = place_ref[index]
        total_ref[place] = total_ref[place] + chunks_ref[index].astype(F32)
        return carry

    lax.fori_loop(0, 192, one, 0, unroll=4)
    keep_ref[...] = total_ref[:64]
    send_ref[...] = total_ref[64:128].astype(BF16)


def upper_kernel(meta_ref, slots_ref, diag_ref, gathered_ref, front_ref, pivot_ref, out_ref, work_ref):
    level, row, col = meta_ref[0], meta_ref[1], meta_ref[2]
    tile = front_ref.shape[1]
    pivot = gathered_ref[:, 0].reshape(tile, tile).astype(F32)
    chosen = gathered_ref[:, 1].reshape(tile, tile).astype(F32)
    front = 4 + level // 4
    solved = eliminate(pivot, chosen, diag_ref[pl.ds(front, 1), :], work_ref).astype(BF16)
    dropped = pivot_slot_of(slots_ref, front) == col
    update = jnp.dot(pivot_ref[...], solved, preferred_element_type=F32)
    result = jnp.where(dropped, 0.0, front_ref[...] - update)
    top = jnp.logical_and(
        lax.broadcasted_iota(jnp.int32, result.shape, 0) < tile // 16, row % 2 == 0
    )
    result = jnp.where(top, 0.0, result).astype(BF16)
    out_ref[...] = result.reshape(out_ref.shape)


def lane_groups(levels):
    groups = []
    for first in range(0, 8, levels):
        for half in range(2):
            groups.append(
                [
                    (first + level) * 8 + 2 * across + half
                    for level in range(levels)
                    for across in range(4)
                ]
            )
    return groups


def exchange(value, levels):
    return lax.all_to_all(
        value,
        ("level", "row"),
        split_axis=0,
        concat_axis=0,
        axis_index_groups=lane_groups(levels),
        tiled=True,
    )


def crossed(value):
    return lax.ppermute(value, "row", [(row, row ^ 1) for row in range(8)])


def spread_columns(value, slot):
    pieces = value.reshape(8, -1, value.shape[-1])
    pieces = lax.all_to_all(pieces, "col", split_axis=0, concat_axis=0, tiled=True)
    piece = lax.dynamic_index_in_dim(pieces, slot, 0, keepdims=True)
    pieces = lax.all_to_all(
        jnp.broadcast_to(piece, pieces.shape), "col", split_axis=0, concat_axis=0, tiled=True
    )
    return pieces.reshape(value.shape)


def body(leaf_blocks, leaf_tiles, leaf_maps, upper_maps, front_slots, pivot_diag):
    tile = leaf_blocks.shape[2]
    level = lax.axis_index("level")
    row = lax.axis_index("row")
    col = lax.axis_index("col")
    meta = jnp.stack([level, row, col]).astype(jnp.int32)
    positions = jnp.arange(8, dtype=jnp.int32)
    slots = jnp.sum(jnp.where(front_slots == 0, positions[None, :], 0), axis=1)
    lower_slot = lax.dynamic_index_in_dim(slots, level // 2, keepdims=False)
    upper_slot = lax.dynamic_index_in_dim(slots, 4 + level // 4, keepdims=False)
    upper_place = lax.dynamic_slice(front_slots, (4 + level // 4, col), (1, 1))[0, 0]
    eighth, sixteenth = tile // 8, tile // 16
    own = leaf_blocks.reshape(12, tile, tile)

    place = call(
        plan_kernel,
        jax.ShapeDtypeStruct((192,), jnp.int32),
        [SMEM] * 4,
        SMEM,
    )(meta, leaf_tiles, leaf_maps, upper_maps)

    pivot_column = spread_columns(own, lower_slot)
    picked = call(
        pick_kernel,
        jax.ShapeDtypeStruct((8, 2, eighth, tile), BF16),
        [SMEM] * 4 + [VMEM],
        VMEM,
        moved=2**21,
    )(meta, leaf_tiles, leaf_maps, front_slots, pivot_column)
    parts = jnp.sum(exchange(picked, 2).astype(F32), axis=0)
    parts = parts + crossed(parts.astype(BF16)).astype(F32)
    gathered = exchange(jnp.broadcast_to(parts.astype(BF16)[None], picked.shape), 2)
    routed = call(
        lower_kernel,
        jax.ShapeDtypeStruct((16, 12, sixteenth, tile), BF16),
        [SMEM, SMEM, VMEM, VMEM, VMEM, VMEM],
        VMEM,
        [pltpu.VMEM((tile, 2 * tile), F32)],
        flops=2**30,
        moved=2**23,
    )(meta, front_slots, pivot_diag, gathered, own, pivot_column)
    chunks = exchange(routed, 4).reshape(192, sixteenth, tile)
    keep, send = call(
        sum_kernel,
        (
            jax.ShapeDtypeStruct((64, sixteenth, tile), F32),
            jax.ShapeDtypeStruct((64, sixteenth, tile), BF16),
        ),
        [SMEM, VMEM],
        None,
        [pltpu.VMEM((129, sixteenth, tile), F32)],
        moved=2**22,
    )(place, chunks)
    front = keep + crossed(send).astype(F32)

    rounded = front.astype(BF16)
    pivot_column = spread_columns(rounded, upper_slot)
    parts = jnp.stack(
        [pivot_column[0], lax.dynamic_index_in_dim(pivot_column, upper_place * 8, 0, keepdims=False)]
    )
    parts = jnp.where(row % 2 == 0, parts, crossed(parts))
    gathered = exchange(jnp.broadcast_to(parts[None], (16,) + parts.shape), 4)
    finished = call(
        upper_kernel,
        jax.ShapeDtypeStruct((16, 4, sixteenth, tile), BF16),
        [SMEM, SMEM, VMEM, VMEM, VMEM, VMEM],
        VMEM,
        [pltpu.VMEM((tile, 2 * tile), F32)],
        flops=2**28,
        moved=2**22,
    )(
        meta,
        front_slots,
        pivot_diag,
        gathered,
        front.reshape(-1, tile),
        pivot_column.reshape(-1, tile),
    )
    result = exchange(finished, 4)
    return jnp.swapaxes(result, 0, 1).reshape(1, -1, tile)


def solution(mesh):
    return jax.shard_map(
        body,
        mesh=mesh,
        in_specs=(P("level", "row", "col"), P(), P(), P(), P(), P()),
        out_specs=P("level", "row", "col"),
        check_vma=False,
    )
```

```python
import functools

import jax
import jax.numpy as jnp
from jax import lax
from jax.experimental import pallas as pl
from jax.experimental.pallas import tpu as pltpu
from jax.sharding import PartitionSpec as P

TILE = 256
NPT = 128
STEP = 32
GROUP = 128
AHEAD = 3
HIGHEST = lax.Precision.HIGHEST
VMEM = pltpu.VMEM
SMEM = pltpu.SMEM
INTERPRET = False
F32 = jnp.float32
BF16 = jnp.bfloat16


def call(kernel, out_shape, in_spaces, out_space=None, scratch=(), flops=0, moved=0):
    return pl.pallas_call(
        kernel,
        out_shape=out_shape,
        in_specs=[pl.BlockSpec(memory_space=space) for space in in_spaces],
        out_specs=pl.BlockSpec(memory_space=out_space)
        if out_space is not None
        else [pl.BlockSpec(memory_space=VMEM) for _ in out_shape],
        scratch_shapes=list(scratch),
        compiler_params=pltpu.CompilerParams(vmem_limit_bytes=32 * 2**20),
        cost_estimate=pl.CostEstimate(flops=flops, bytes_accessed=moved, transcendentals=0),
        interpret=INTERPRET,
    )


def plan_kernel(meta_ref, tiles_ref, leaf_maps_ref, upper_maps_ref, place_ref):
    level, row = meta_ref[0], meta_ref[1]
    half = row % 2
    base = level // 4 * 4

    def one(index, carry):
        source, tile = index // 12, index % 12
        quad, across = source // 4, source % 4
        leaf = base + quad
        leaf_tile = (2 * across + half) * 12 + tile
        lower_tile = leaf_maps_ref[leaf, leaf_tile]
        upper_tile = upper_maps_ref[leaf // 2, lower_tile]
        kept = jnp.logical_and(leaf_tile < tiles_ref[leaf], lower_tile != 0)
        home_row = upper_tile // 4 % 8
        position = (upper_tile // 32 * 4 + home_row // 2) * 4 + upper_tile % 4
        other = (home_row % 2 != half).astype(jnp.int32)
        place_ref[index] = jnp.where(kept, position + 64 * other, 128)
        return carry

    lax.fori_loop(0, 192, one, 0)


def share_kernel(meta_ref, tiles_ref, leaf_maps_ref, leaf_ref, out_ref):
    level, row = meta_ref[0], meta_ref[1]
    tile = leaf_ref.shape[1]
    across, rows = out_ref.shape[0], out_ref.shape[2]
    out_ref[...] = jnp.zeros_like(out_ref)

    def look(index, carry):
        leaf_tile = row * 12 + index
        lower_tile = leaf_maps_ref[level, leaf_tile]
        match = jnp.logical_and(lower_tile % 16 == 0, leaf_tile < tiles_ref[level])

        @pl.when(match)
        def _():
            out_ref[:, lower_tile // 16] = leaf_ref[index].reshape(across, rows, tile)

        return carry

    lax.fori_loop(0, 12, look, 0)


def combine_kernel(meta_ref, slots_ref, shares_ref, out_ref, total_ref):
    front = meta_ref[0] // 2
    total = shares_ref[0].astype(F32)
    for source in range(1, shares_ref.shape[0]):
        total = total + shares_ref[source].astype(F32)
    total_ref[...] = total.astype(BF16)
    for column in range(8):
        out_ref[column, 0] = total_ref[0]
        out_ref[column, 1] = total_ref[slots_ref[front, column]]


def split(value):
    high = value.astype(BF16).astype(F32)
    return high, value - high


def dot3(left, right, dims):
    left_high, left_low = (part.astype(BF16) for part in split(left))
    right_high, right_low = (part.astype(BF16) for part in split(right))
    product = functools.partial(
        lax.dot_general, dimension_numbers=(dims, ((), ())), preferred_element_type=F32
    )
    return (product(left_low, right_high) + product(left_high, right_low)) + product(
        left_high, right_high
    )


def invert(work_ref):
    tile = work_ref.shape[0]
    group = min(GROUP, tile)
    groups = tile // group
    ids = lax.broadcasted_iota(jnp.int32, (STEP, group), 0)
    lanes = lax.broadcasted_iota(jnp.int32, (1, group), 1)
    for start in range(0, tile, STEP):
        own = start // group
        offset = start - own * group
        rows = slice(start, start + STEP)
        block = [work_ref[rows, k * group : (k + 1) * group] for k in range(groups)]

        def column(step):
            lane = offset + step
            return jnp.broadcast_to(block[own][:, lane : lane + 1], (STEP, group))

        ahead = [column(step) for step in range(AHEAD)]
        for step in range(STEP):
            if step + AHEAD < STEP:
                ahead.append(column(step + AHEAD))
            here = ahead.pop(0)
            inverse = 1.0 / here[step : step + 1]
            pivot_row = ids == step
            pivot_lane = lanes == offset + step
            for k in range(len(ahead)):
                scaled = ahead[k][step : step + 1] * inverse
                ahead[k] = jnp.where(pivot_row, scaled, ahead[k] - here * scaled)
            for k in range(groups):
                value = block[k]
                scaled = value[step : step + 1]
                if k == own:
                    scaled = jnp.where(pivot_lane, 1.0, scaled)
                    value = jnp.where(pivot_lane, 0.0, value)
                scaled = scaled * inverse
                block[k] = jnp.where(pivot_row, scaled, value - here * scaled)
        factor = work_ref[:, own * group : (own + 1) * group]
        fac_rows = lax.broadcasted_iota(jnp.int32, factor.shape, 0)
        fac_cols = lax.broadcasted_iota(jnp.int32, factor.shape, 1)
        own_row = jnp.logical_and(fac_rows >= start, fac_rows < start + STEP)
        own_col = jnp.logical_and(fac_cols >= offset, fac_cols < offset + STEP)
        work_ref[:, own * group : (own + 1) * group] = jnp.where(own_col, 0.0, factor)
        factor = jnp.where(jnp.logical_and(own_col, jnp.logical_not(own_row)), factor, 0.0)
        whole = jnp.concatenate(block, axis=1)
        if group >= 4 * STEP:
            high, low = split(factor)
            factor = high + pltpu.roll(high, STEP, 1) + pltpu.roll(low, 2 * STEP, 1)
            whole_high, whole_low = (part.astype(BF16) for part in split(whole))
            pieces = [jnp.zeros((STEP, tile), BF16) for _ in range(group // STEP)]
            place = offset // STEP
            for shift, part in enumerate((whole_high, whole_low, whole_high)):
                pieces[(place + shift) % len(pieces)] = part
            update = jnp.dot(
                factor.astype(BF16), jnp.concatenate(pieces, axis=0), preferred_element_type=F32
            )
        else:
            update = jnp.dot(
                factor[:, offset : offset + STEP], whole, precision=HIGHEST, preferred_element_type=F32
            )
        work_ref[...] = work_ref[...] - update
        work_ref[rows, :] = whole


def solve_kernel(front_of, meta_ref, diag_ref, gathered_ref, out_ref, work_ref):
    tile = out_ref.shape[0]
    pivot = gathered_ref[:, 0].reshape(tile, tile).astype(F32)
    chosen = gathered_ref[:, 1].reshape(tile, tile).astype(F32)
    rows = lax.broadcasted_iota(jnp.int32, (tile, tile), 0)
    columns = lax.broadcasted_iota(jnp.int32, (tile, tile), 1)
    diagonal = diag_ref[pl.ds(front_of(meta_ref[0]), 1), :]
    work_ref[...] = (pivot + pivot.T) * 0.5 + jnp.where(rows == columns, diagonal, 0.0)
    invert(work_ref)
    out_ref[...] = dot3(work_ref[...], chosen, ((1,), (1,))).astype(BF16)


def lower_front(level):
    return level // 2


def upper_front(level):
    return 4 + level // 4


def solve(front_of, meta, diagonals, gathered):
    tile = gathered.shape[-1]
    return call(
        functools.partial(solve_kernel, front_of),
        jax.ShapeDtypeStruct((tile, tile), BF16),
        [SMEM, VMEM, VMEM],
        VMEM,
        [pltpu.VMEM((tile, tile), F32)],
        flops=2**29,
        moved=2**22,
    )(meta, diagonals, gathered)


def pivot_slot_of(slots_ref, front):
    slot = jnp.int32(0)
    for index in range(8):
        slot = jnp.where(slots_ref[front, index] == 0, index, slot)
    return slot


def lower_kernel(
    meta_ref, slots_ref, place_ref, chunks_ref, pivot_ref, solved_ref, keep_ref, send_ref, share_ref, total_ref, update_ref
):
    level, row, col = meta_ref[0], meta_ref[1], meta_ref[2]
    total_ref[...] = jnp.zeros_like(total_ref)
    half = chunks_ref.shape[0] // 2
    for child in range(2):
        dropped = pivot_slot_of(slots_ref, level // 4 * 2 + child) == col
        pivot = pivot_ref[child * half : (child + 1) * half]
        update = jnp.dot(
            pivot.reshape(-1, pivot.shape[-1]), solved_ref[child], preferred_element_type=F32
        )
        update_ref[...] = update.reshape(update_ref.shape)

        def one(index, carry):
            place = jnp.where(dropped, 128, place_ref[child * half + index])
            value = chunks_ref[child * half + index].astype(F32) - update_ref[index]
            total_ref[place] = total_ref[place] + value
            return carry

        lax.fori_loop(0, half, one, 0, unroll=4)
    keep_ref[...] = total_ref[:64]
    send_ref[...] = total_ref[64:128].astype(BF16)
    first = row % 2 * 64
    for column in range(8):
        share_ref[column, 0] = total_ref[first].astype(BF16)
        share_ref[column, 1] = total_ref[first + 8 * slots_ref[4 + level // 4, column]].astype(BF16)


def upper_kernel(meta_ref, slots_ref, front_ref, pivot_ref, solved_ref, out_ref):
    level, row, col = meta_ref[0], meta_ref[1], meta_ref[2]
    tile = front_ref.shape[1]
    dropped = pivot_slot_of(slots_ref, 4 + level // 4) == col
    update = jnp.dot(pivot_ref[...], solved_ref[...], preferred_element_type=F32)
    result = jnp.where(dropped, 0.0, front_ref[...] - update)
    top = jnp.logical_and(
        lax.broadcasted_iota(jnp.int32, result.shape, 0) < tile // 16, row % 2 == 0
    )
    result = jnp.where(top, 0.0, result).astype(BF16)
    out_ref[...] = result.reshape(out_ref.shape)


def lane_groups(levels):
    groups = []
    for first in range(0, 8, levels):
        for half in range(2):
            groups.append(
                [
                    (first + level) * 8 + 2 * across + half
                    for level in range(levels)
                    for across in range(4)
                ]
            )
    return groups


def exchange(value, levels):
    return lax.all_to_all(
        value,
        ("level", "row"),
        split_axis=0,
        concat_axis=0,
        axis_index_groups=lane_groups(levels),
        tiled=True,
    )


def crossed(value):
    return lax.ppermute(value, "row", [(row, row ^ 1) for row in range(8)])


def over_columns(value):
    return lax.all_to_all(value, "col", split_axis=0, concat_axis=0, tiled=True)


def spread_columns(value, slot):
    pieces = over_columns(value.reshape(8, -1, value.shape[-1]))
    piece = lax.dynamic_index_in_dim(pieces, slot, 0, keepdims=True)
    return over_columns(jnp.broadcast_to(piece, pieces.shape)).reshape(value.shape)


def gather_tiles(shares, slot, levels):
    parts = lax.dynamic_index_in_dim(over_columns(shares), slot, 0, keepdims=False)
    parts = (parts.astype(F32) + crossed(parts).astype(F32)).astype(BF16)
    return exchange(jnp.broadcast_to(parts[None], (4 * levels,) + parts.shape), levels)


def body(leaf_blocks, leaf_tiles, leaf_maps, upper_maps, front_slots, pivot_diag):
    tile = leaf_blocks.shape[2]
    level = lax.axis_index("level")
    row = lax.axis_index("row")
    col = lax.axis_index("col")
    meta = jnp.stack([level, row, col]).astype(jnp.int32)
    positions = jnp.arange(8, dtype=jnp.int32)
    slots = jnp.sum(jnp.where(front_slots == 0, positions[None, :], 0), axis=1)

    def slot_of(front):
        return lax.dynamic_index_in_dim(slots, front, keepdims=False)

    eighth, sixteenth = tile // 8, tile // 16
    own = leaf_blocks.reshape(12, tile, tile)

    shares = call(
        share_kernel,
        jax.ShapeDtypeStruct((8, 8, eighth, tile), BF16),
        [SMEM] * 3 + [VMEM],
        VMEM,
        moved=2**21,
    )(meta, leaf_tiles, leaf_maps, own)
    shares = exchange(shares, 2)
    chunks = jnp.swapaxes(own.reshape(12, 16, sixteenth, tile), 0, 1)
    chunks = exchange(chunks, 4).reshape(192, sixteenth, tile)
    place = call(
        plan_kernel,
        jax.ShapeDtypeStruct((192,), jnp.int32),
        [SMEM] * 4,
        SMEM,
    )(meta, leaf_tiles, leaf_maps, upper_maps)
    shares = call(
        combine_kernel,
        jax.ShapeDtypeStruct((8, 2, eighth, tile), BF16),
        [SMEM, SMEM, VMEM],
        VMEM,
        [pltpu.VMEM((8, eighth, tile), BF16)],
        moved=2**21,
    )(meta, front_slots, shares)
    gathered = gather_tiles(shares, slot_of(level // 2), 2)
    pivot_columns = spread_columns(chunks, slot_of(level // 4 * 2 + col // 4))
    solved = solve(lower_front, meta, pivot_diag, gathered)
    other = lax.ppermute(solved, "level", [(index, index ^ 2) for index in range(8)])
    first_child = level // 2 % 2 == 0
    solved = jnp.where(first_child, jnp.stack([solved, other]), jnp.stack([other, solved]))
    keep, send, shares = call(
        lower_kernel,
        (
            jax.ShapeDtypeStruct((64, sixteenth, tile), F32),
            jax.ShapeDtypeStruct((64, sixteenth, tile), BF16),
            jax.ShapeDtypeStruct((8, 2, sixteenth, tile), BF16),
        ),
        [SMEM, SMEM, SMEM, VMEM, VMEM, VMEM],
        None,
        [pltpu.VMEM((129, sixteenth, tile), F32), pltpu.VMEM((96, sixteenth, tile), F32)],
        flops=2**29,
        moved=2**23,
    )(meta, front_slots, place, chunks, pivot_columns, solved)

    upper_slot = slot_of(4 + level // 4)
    gathered = gather_tiles(shares, upper_slot, 4)
    front = keep + crossed(send).astype(F32)
    pivot_columns = spread_columns(front.astype(BF16), upper_slot)
    solved = solve(upper_front, meta, pivot_diag, gathered)
    finished = call(
        upper_kernel,
        jax.ShapeDtypeStruct((16, 4, sixteenth, tile), BF16),
        [SMEM, SMEM, VMEM, VMEM, VMEM],
        VMEM,
        flops=2**28,
        moved=2**22,
    )(meta, front_slots, front.reshape(-1, tile), pivot_columns.reshape(-1, tile), solved)
    result = exchange(finished, 4)
    return jnp.swapaxes(result, 0, 1).reshape(1, -1, tile)


def solution(mesh):
    return jax.shard_map(
        body,
        mesh=mesh,
        in_specs=(P("level", "row", "col"), P(), P(), P(), P(), P()),
        out_specs=P("level", "row", "col"),
        check_vma=False,
    )
```

```python
import functools

import jax
import jax.numpy as jnp
from jax import lax
from jax.experimental import pallas as pl
from jax.experimental.pallas import tpu as pltpu
from jax.sharding import PartitionSpec as P

TILE = 256
NPT = 128
STEP = 32
GROUP = 128
AHEAD = 3
HIGHEST = lax.Precision.HIGHEST
VMEM = pltpu.VMEM
SMEM = pltpu.SMEM
INTERPRET = False
F32 = jnp.float32
BF16 = jnp.bfloat16


def call(kernel, out_shape, in_spaces, out_space=None, scratch=(), flops=0, moved=0):
    return pl.pallas_call(
        kernel,
        out_shape=out_shape,
        in_specs=[pl.BlockSpec(memory_space=space) for space in in_spaces],
        out_specs=pl.BlockSpec(memory_space=out_space)
        if out_space is not None
        else [pl.BlockSpec(memory_space=VMEM) for _ in out_shape],
        scratch_shapes=list(scratch),
        compiler_params=pltpu.CompilerParams(vmem_limit_bytes=32 * 2**20),
        cost_estimate=pl.CostEstimate(flops=flops, bytes_accessed=moved, transcendentals=0),
        interpret=INTERPRET,
    )


def plan_kernel(meta_ref, tiles_ref, leaf_maps_ref, upper_maps_ref, place_ref):
    half = meta_ref[1] & 1
    base = meta_ref[0] & 4
    for source in range(16):
        leaf = base + source // 4
        front = (base >> 1) + source // 8
        live = tiles_ref[leaf]
        first = (2 * (source % 4) + half) * 12
        for tile in range(12):
            lower_tile = leaf_maps_ref[leaf, first + tile]
            upper_tile = upper_maps_ref[front, lower_tile]
            home_row = (upper_tile >> 2) & 7
            position = ((upper_tile >> 5) << 4) + ((home_row >> 1) << 2) + (upper_tile & 3)
            position = position + (((home_row & 1) ^ half) << 6)
            kept = jnp.logical_and(first + tile < live, lower_tile != 0)
            place_ref[source * 12 + tile] = jnp.where(kept, position, 128)


def share_kernel(meta_ref, tiles_ref, leaf_maps_ref, leaf_ref, out_ref):
    level, row = meta_ref[0], meta_ref[1]
    tile = leaf_ref.shape[1]
    across, rows = out_ref.shape[0], out_ref.shape[2]
    out_ref[...] = jnp.zeros_like(out_ref)

    def look(index, carry):
        leaf_tile = row * 12 + index
        lower_tile = leaf_maps_ref[level, leaf_tile]
        match = jnp.logical_and(lower_tile % 16 == 0, leaf_tile < tiles_ref[level])

        @pl.when(match)
        def _():
            out_ref[:, lower_tile // 16] = leaf_ref[index].reshape(across, rows, tile)

        return carry

    lax.fori_loop(0, 12, look, 0)


def combine_kernel(shares_ref, out_ref):
    total = shares_ref[0].astype(F32)
    for source in range(1, shares_ref.shape[0]):
        total = total + shares_ref[source].astype(F32)
    out_ref[...] = total.astype(BF16)


def split(value):
    high = value.astype(BF16).astype(F32)
    return high, value - high


def dot3(left, right, dims):
    left_high, left_low = (part.astype(BF16) for part in split(left))
    right_high, right_low = (part.astype(BF16) for part in split(right))
    product = functools.partial(
        lax.dot_general, dimension_numbers=(dims, ((), ())), preferred_element_type=F32
    )
    return (product(left_low, right_high) + product(left_high, right_low)) + product(
        left_high, right_high
    )


def invert(work_ref):
    tile = work_ref.shape[0]
    group = min(GROUP, tile)
    groups = tile // group
    ids = lax.broadcasted_iota(jnp.int32, (STEP, group), 0)
    lanes = lax.broadcasted_iota(jnp.int32, (1, group), 1)
    for start in range(0, tile, STEP):
        own = start // group
        offset = start - own * group
        rows = slice(start, start + STEP)
        block = [work_ref[rows, k * group : (k + 1) * group] for k in range(groups)]

        def column(step):
            lane = offset + step
            return jnp.broadcast_to(block[own][:, lane : lane + 1], (STEP, group))

        ahead = [column(step) for step in range(AHEAD)]
        for step in range(STEP):
            if step + AHEAD < STEP:
                ahead.append(column(step + AHEAD))
            here = ahead.pop(0)
            inverse = 1.0 / here[step : step + 1]
            pivot_row = ids == step
            pivot_lane = lanes == offset + step
            for k in range(len(ahead)):
                scaled = ahead[k][step : step + 1] * inverse
                ahead[k] = jnp.where(pivot_row, scaled, ahead[k] - here * scaled)
            for k in range(groups):
                value = block[k]
                scaled = value[step : step + 1]
                if k == own:
                    scaled = jnp.where(pivot_lane, 1.0, scaled)
                    value = jnp.where(pivot_lane, 0.0, value)
                scaled = scaled * inverse
                block[k] = jnp.where(pivot_row, scaled, value - here * scaled)
        factor = work_ref[:, own * group : (own + 1) * group]
        fac_rows = lax.broadcasted_iota(jnp.int32, factor.shape, 0)
        fac_cols = lax.broadcasted_iota(jnp.int32, factor.shape, 1)
        own_row = jnp.logical_and(fac_rows >= start, fac_rows < start + STEP)
        own_col = jnp.logical_and(fac_cols >= offset, fac_cols < offset + STEP)
        work_ref[:, own * group : (own + 1) * group] = jnp.where(own_col, 0.0, factor)
        factor = jnp.where(jnp.logical_and(own_col, jnp.logical_not(own_row)), factor, 0.0)
        whole = jnp.concatenate(block, axis=1)
        if group >= 4 * STEP:
            high, low = split(factor)
            factor = high + pltpu.roll(high, STEP, 1) + pltpu.roll(low, 2 * STEP, 1)
            whole_high, whole_low = (part.astype(BF16) for part in split(whole))
            pieces = [jnp.zeros((STEP, tile), BF16) for _ in range(group // STEP)]
            place = offset // STEP
            for shift, part in enumerate((whole_high, whole_low, whole_high)):
                pieces[(place + shift) % len(pieces)] = part
            update = jnp.dot(
                factor.astype(BF16), jnp.concatenate(pieces, axis=0), preferred_element_type=F32
            )
        else:
            update = jnp.dot(
                factor[:, offset : offset + STEP], whole, precision=HIGHEST, preferred_element_type=F32
            )
        work_ref[...] = work_ref[...] - update
        work_ref[rows, :] = whole


def solve_kernel(front_of, place_of, meta_ref, diag_ref, gathered_ref, out_ref, work_ref, chosen_ref):
    tile = out_ref.shape[0]
    count, length = gathered_ref.shape[0], gathered_ref.shape[2]
    place = place_of(meta_ref)
    for piece in range(count):
        rows = pl.ds(pl.multiple_of((place ^ piece) * length, length), length)
        work_ref[rows, :] = gathered_ref[piece, 0].astype(F32)
        chosen_ref[rows, :] = gathered_ref[piece, 1].astype(F32)
    pivot = work_ref[...]
    rows = lax.broadcasted_iota(jnp.int32, (tile, tile), 0)
    columns = lax.broadcasted_iota(jnp.int32, (tile, tile), 1)
    diagonal = diag_ref[pl.ds(front_of(meta_ref[0]), 1), :]
    work_ref[...] = (pivot + pivot.T) * 0.5 + jnp.where(rows == columns, diagonal, 0.0)
    invert(work_ref)
    out_ref[...] = dot3(work_ref[...], chosen_ref[...], ((1,), (1,))).astype(BF16)


def lower_front(level):
    return level // 2


def upper_front(level):
    return 4 + level // 4


def pair_place(meta_ref):
    return (meta_ref[0] & 1) * 4 + (meta_ref[1] >> 1)


def no_place(meta_ref):
    return jnp.int32(0)


def solve(front_of, place_of, meta, diagonals, gathered):
    tile = gathered.shape[-1]
    return call(
        functools.partial(solve_kernel, front_of, place_of),
        jax.ShapeDtypeStruct((tile, tile), BF16),
        [SMEM, VMEM, VMEM],
        VMEM,
        [pltpu.VMEM((tile, tile), F32), pltpu.VMEM((tile, tile), F32)],
        flops=2**29,
        moved=2**22,
    )(meta, diagonals, gathered)


def pivot_slot_of(slots_ref, front):
    slot = jnp.int32(0)
    for index in range(8):
        slot = jnp.where(slots_ref[front, index] == 0, index, slot)
    return slot


def lower_kernel(
    meta_ref, slots_ref, place_ref, chunks_ref, pivot_ref, solved_ref, keep_ref, send_ref, spread_ref, total_ref, update_ref
):
    level, row, col = meta_ref[0], meta_ref[1], meta_ref[2]
    total_ref[...] = jnp.zeros_like(total_ref)
    half = chunks_ref.shape[0] // 2
    for child in range(2):
        dropped = pivot_slot_of(slots_ref, level // 4 * 2 + child) == col
        pivot = pivot_ref[child * half : (child + 1) * half]
        update = jnp.dot(
            pivot.reshape(-1, pivot.shape[-1]), solved_ref[child], preferred_element_type=F32
        )
        update_ref[...] = update.reshape(update_ref.shape)

        def one(index, carry):
            place = jnp.where(dropped, 128, place_ref[child * half + index])
            value = chunks_ref[child * half + index].astype(F32) - update_ref[index]
            total_ref[place] = total_ref[place] + value
            return carry

        lax.fori_loop(0, half, one, 0, unroll=4)
    keep_ref[...] = total_ref[:64]
    send_ref[...] = total_ref[64:128].astype(BF16)
    first = row % 2 * 64
    length, tile = total_ref.shape[1], total_ref.shape[2]
    for column in range(8):
        for part in range(2):
            value = total_ref[part * 64 + column * 8 : part * 64 + column * 8 + 8]
            spread_ref[column, part * 8 * length : (part + 1) * 8 * length] = value.astype(
                BF16
            ).reshape(8 * length, tile)
        panel_tile = first + 8 * slots_ref[4 + level // 4, column]
        spread_ref[column, 16 * length : 17 * length] = total_ref[first].astype(BF16)
        spread_ref[column, 17 * length : 18 * length] = total_ref[panel_tile].astype(BF16)


def upper_kernel(meta_ref, slots_ref, keep_ref, sent_ref, pivot_ref, solved_ref, out_ref):
    level, row, col = meta_ref[0], meta_ref[1], meta_ref[2]
    tile = keep_ref.shape[1]
    dropped = pivot_slot_of(slots_ref, 4 + level // 4) == col
    update = jnp.dot(pivot_ref[...], solved_ref[...], preferred_element_type=F32)
    front = keep_ref[...] + sent_ref[...].astype(F32)
    result = jnp.where(dropped, 0.0, front - update)
    top = jnp.logical_and(
        lax.broadcasted_iota(jnp.int32, result.shape, 0) < tile // 16, row % 2 == 0
    )
    result = jnp.where(top, 0.0, result).astype(BF16)
    out_ref[...] = result.reshape(out_ref.shape)


def lane_groups(levels):
    groups = []
    for first in range(0, 8, levels):
        for half in range(2):
            groups.append(
                [
                    (first + level) * 8 + 2 * across + half
                    for level in range(levels)
                    for across in range(4)
                ]
            )
    return groups


def exchange(value, levels):
    return lax.all_to_all(
        value,
        ("level", "row"),
        split_axis=0,
        concat_axis=0,
        axis_index_groups=lane_groups(levels),
        tiled=True,
    )


def over_columns(value):
    return lax.all_to_all(value, "col", split_axis=0, concat_axis=0, tiled=True)


def swapped(value, axis, mask):
    return lax.ppermute(value, axis, [(index, index ^ mask) for index in range(8)])


def tied(first, second):
    return lax.optimization_barrier((first, second))


def picked(pieces, slot):
    return lax.dynamic_index_in_dim(pieces, slot, 0, keepdims=False)


def repeated(value, count):
    return jnp.broadcast_to(value[None], (count,) + value.shape)


def body(leaf_blocks, leaf_tiles, leaf_maps, upper_maps, front_slots, pivot_diag):
    tile = leaf_blocks.shape[2]
    level = lax.axis_index("level")
    row = lax.axis_index("row")
    col = lax.axis_index("col")
    meta = jnp.stack([level, row, col]).astype(jnp.int32)
    positions = jnp.arange(8, dtype=jnp.int32)
    slots = jnp.sum(jnp.where(front_slots == 0, positions[None, :], 0), axis=1)
    eighth, sixteenth = tile // 8, tile // 16
    own = leaf_blocks.reshape(12, tile, tile)

    shares = call(
        share_kernel,
        jax.ShapeDtypeStruct((8, 8, eighth, tile), BF16),
        [SMEM] * 3 + [VMEM],
        VMEM,
        moved=2**21,
    )(meta, leaf_tiles, leaf_maps, own)
    shares = exchange(shares, 2)
    chunks = jnp.swapaxes(own.reshape(12, 16, sixteenth, tile), 0, 1)
    chunks, shares = tied(chunks, shares)
    chunks = exchange(chunks, 4).reshape(8, -1, tile)
    place = call(
        plan_kernel,
        jax.ShapeDtypeStruct((192,), jnp.int32),
        [SMEM] * 4,
        SMEM,
    )(meta, leaf_tiles, leaf_maps, upper_maps)

    shares = call(
        combine_kernel,
        jax.ShapeDtypeStruct((8, eighth, tile), BF16),
        [VMEM],
        VMEM,
        moved=2**21,
    )(shares)
    away = col ^ picked(slots, level // 2)
    for mask in (1, 2, 4):
        shares = jnp.where(away & mask == 0, shares, swapped(shares, "col", mask))
    my_tile = lax.dynamic_slice(front_slots, (level // 2, col), (1, 1))[0, 0]
    parts = jnp.stack([shares[0], picked(shares, my_tile)])
    parts = (parts.astype(F32) + swapped(parts, "row", 1).astype(F32)).astype(BF16)

    chunks, parts = tied(chunks, parts)
    pieces = over_columns(chunks)
    gathered = parts[None]
    for axis, mask in (("row", 2), ("row", 4), ("level", 1)):
        gathered = jnp.concatenate([gathered, swapped(gathered, axis, mask)], axis=0)
    piece = picked(pieces, picked(slots, level // 4 * 2 + col // 4))
    piece, gathered = tied(piece, gathered)
    pivot_columns = over_columns(repeated(piece, 8)).reshape(192, sixteenth, tile)
    solved = solve(lower_front, pair_place, meta, pivot_diag, gathered)
    other = swapped(solved, "level", 2)
    first_child = level // 2 % 2 == 0
    solved = jnp.where(first_child, jnp.stack([solved, other]), jnp.stack([other, solved]))
    keep, send, spread = call(
        lower_kernel,
        (
            jax.ShapeDtypeStruct((64, sixteenth, tile), F32),
            jax.ShapeDtypeStruct((64, sixteenth, tile), BF16),
            jax.ShapeDtypeStruct((8, 18 * sixteenth, tile), BF16),
        ),
        [SMEM, SMEM, SMEM, VMEM, VMEM, VMEM],
        None,
        [pltpu.VMEM((129, sixteenth, tile), F32), pltpu.VMEM((96, sixteenth, tile), F32)],
        flops=2**29,
        moved=2**23,
    )(meta, front_slots, place, chunks.reshape(192, sixteenth, tile), pivot_columns, solved)

    spread = picked(over_columns(spread), picked(slots, 4 + level // 4)).astype(F32)
    passed = swapped(spread[8 * sixteenth :].astype(BF16), "row", 1).astype(F32)
    piece = (spread[: 8 * sixteenth] + passed[: 8 * sixteenth]).astype(BF16)
    parts = (spread[16 * sixteenth :] + passed[8 * sixteenth :]).astype(BF16)
    gathered = exchange(repeated(parts.reshape(2, sixteenth, tile), 16), 4)
    piece, gathered = tied(piece, gathered)
    pivot_columns = over_columns(repeated(piece, 8)).reshape(-1, tile)
    solved = solve(upper_front, no_place, meta, pivot_diag, gathered)
    sent = swapped(send, "row", 1)
    finished = call(
        upper_kernel,
        jax.ShapeDtypeStruct((16, 4, sixteenth, tile), BF16),
        [SMEM, SMEM, VMEM, VMEM, VMEM, VMEM],
        VMEM,
        flops=2**28,
        moved=2**22,
    )(
        meta,
        front_slots,
        keep.reshape(-1, tile),
        sent.reshape(-1, tile),
        pivot_columns,
        solved,
    )
    result = exchange(finished, 4)
    return jnp.swapaxes(result, 0, 1).reshape(1, -1, tile)


def solution(mesh):
    return jax.shard_map(
        body,
        mesh=mesh,
        in_specs=(P("level", "row", "col"), P(), P(), P(), P(), P()),
        out_specs=P("level", "row", "col"),
        check_vma=False,
    )
```

```python
import functools

import jax
import jax.numpy as jnp
from jax import lax
from jax.experimental import pallas as pl
from jax.experimental.pallas import tpu as pltpu
from jax.sharding import PartitionSpec as P

TILE = 256
NPT = 128
STEP = 32
GROUP = 128
AHEAD = 3
HIGHEST = lax.Precision.HIGHEST
VMEM = pltpu.VMEM
SMEM = pltpu.SMEM
INTERPRET = False
F32 = jnp.float32
BF16 = jnp.bfloat16


def call(kernel, out_shape, in_spaces, out_space=None, scratch=(), flops=0, moved=0):
    return pl.pallas_call(
        kernel,
        out_shape=out_shape,
        in_specs=[pl.BlockSpec(memory_space=space) for space in in_spaces],
        out_specs=pl.BlockSpec(memory_space=out_space)
        if out_space is not None
        else [pl.BlockSpec(memory_space=VMEM) for _ in out_shape],
        scratch_shapes=list(scratch),
        compiler_params=pltpu.CompilerParams(vmem_limit_bytes=32 * 2**20),
        cost_estimate=pl.CostEstimate(flops=flops, bytes_accessed=moved, transcendentals=0),
        interpret=INTERPRET,
    )


def plan_kernel(meta_ref, tiles_ref, leaf_maps_ref, upper_maps_ref, place_ref):
    half = meta_ref[1] & 1
    base = meta_ref[0] & 4
    for source in range(16):
        leaf = base + source // 4
        front = (base >> 1) + source // 8
        live = tiles_ref[leaf]
        first = (2 * (source % 4) + half) * 12
        for tile in range(12):
            lower_tile = leaf_maps_ref[leaf, first + tile]
            upper_tile = upper_maps_ref[front, lower_tile]
            home_row = (upper_tile >> 2) & 7
            position = ((upper_tile >> 5) << 4) + ((home_row >> 1) << 2) + (upper_tile & 3)
            position = position + (((home_row & 1) ^ half) << 6)
            kept = jnp.logical_and(first + tile < live, lower_tile != 0)
            place_ref[source * 12 + tile] = jnp.where(kept, position, 128)


def share_kernel(meta_ref, tiles_ref, leaf_maps_ref, leaf_ref, out_ref):
    level, row = meta_ref[0], meta_ref[1]
    tile = leaf_ref.shape[1]
    across, rows = out_ref.shape[0], out_ref.shape[2]
    out_ref[...] = jnp.zeros_like(out_ref)

    def look(index, carry):
        leaf_tile = row * 12 + index
        lower_tile = leaf_maps_ref[level, leaf_tile]
        match = jnp.logical_and(lower_tile % 16 == 0, leaf_tile < tiles_ref[level])

        @pl.when(match)
        def _():
            out_ref[:, lower_tile // 16] = leaf_ref[index].reshape(across, rows, tile)

        return carry

    lax.fori_loop(0, 12, look, 0)


def combine_kernel(shares_ref, out_ref):
    total = shares_ref[0].astype(F32)
    for source in range(1, shares_ref.shape[0]):
        total = total + shares_ref[source].astype(F32)
    out_ref[...] = total.astype(BF16)


def split(value):
    high = value.astype(BF16).astype(F32)
    return high, value - high


def dot3(left, right, dims):
    left_high, left_low = (part.astype(BF16) for part in split(left))
    right_high, right_low = (part.astype(BF16) for part in split(right))
    product = functools.partial(
        lax.dot_general, dimension_numbers=(dims, ((), ())), preferred_element_type=F32
    )
    return (product(left_low, right_high) + product(left_high, right_low)) + product(
        left_high, right_high
    )


def invert(work_ref):
    tile = work_ref.shape[0]
    group = min(GROUP, tile)
    groups = tile // group
    ids = lax.broadcasted_iota(jnp.int32, (STEP, group), 0)
    lanes = lax.broadcasted_iota(jnp.int32, (1, group), 1)
    for start in range(0, tile, STEP):
        own = start // group
        offset = start - own * group
        rows = slice(start, start + STEP)
        block = [work_ref[rows, k * group : (k + 1) * group] for k in range(groups)]

        def column(step):
            lane = offset + step
            return jnp.broadcast_to(block[own][:, lane : lane + 1], (STEP, group))

        ahead = [column(step) for step in range(AHEAD)]
        for step in range(STEP):
            if step + AHEAD < STEP:
                ahead.append(column(step + AHEAD))
            here = ahead.pop(0)
            inverse = 1.0 / here[step : step + 1]
            pivot_row = ids == step
            pivot_lane = lanes == offset + step
            for k in range(len(ahead)):
                scaled = ahead[k][step : step + 1] * inverse
                ahead[k] = jnp.where(pivot_row, scaled, ahead[k] - here * scaled)
            for k in range(groups):
                value = block[k]
                scaled = value[step : step + 1]
                if k == own:
                    scaled = jnp.where(pivot_lane, 1.0, scaled)
                    value = jnp.where(pivot_lane, 0.0, value)
                scaled = scaled * inverse
                block[k] = jnp.where(pivot_row, scaled, value - here * scaled)
        factor = work_ref[:, own * group : (own + 1) * group]
        fac_rows = lax.broadcasted_iota(jnp.int32, factor.shape, 0)
        fac_cols = lax.broadcasted_iota(jnp.int32, factor.shape, 1)
        own_row = jnp.logical_and(fac_rows >= start, fac_rows < start + STEP)
        own_col = jnp.logical_and(fac_cols >= offset, fac_cols < offset + STEP)
        work_ref[:, own * group : (own + 1) * group] = jnp.where(own_col, 0.0, factor)
        factor = jnp.where(jnp.logical_and(own_col, jnp.logical_not(own_row)), factor, 0.0)
        whole = jnp.concatenate(block, axis=1)
        if group >= 4 * STEP:
            high, low = split(factor)
            factor = high + pltpu.roll(high, STEP, 1) + pltpu.roll(low, 2 * STEP, 1)
            whole_high, whole_low = (part.astype(BF16) for part in split(whole))
            pieces = [jnp.zeros((STEP, tile), BF16) for _ in range(group // STEP)]
            place = offset // STEP
            for shift, part in enumerate((whole_high, whole_low, whole_high)):
                pieces[(place + shift) % len(pieces)] = part
            update = jnp.dot(
                factor.astype(BF16), jnp.concatenate(pieces, axis=0), preferred_element_type=F32
            )
        else:
            update = jnp.dot(
                factor[:, offset : offset + STEP], whole, precision=HIGHEST, preferred_element_type=F32
            )
        work_ref[...] = work_ref[...] - update
        work_ref[rows, :] = whole


def solve_kernel(front_of, place_of, meta_ref, diag_ref, gathered_ref, out_ref, work_ref, chosen_ref):
    tile = out_ref.shape[0]
    count, length = gathered_ref.shape[0], gathered_ref.shape[2]
    place = place_of(meta_ref)
    for piece in range(count):
        rows = pl.ds(pl.multiple_of((place ^ piece) * length, length), length)
        work_ref[rows, :] = gathered_ref[piece, 0].astype(F32)
        chosen_ref[rows, :] = gathered_ref[piece, 1].astype(F32)
    pivot = work_ref[...]
    rows = lax.broadcasted_iota(jnp.int32, (tile, tile), 0)
    columns = lax.broadcasted_iota(jnp.int32, (tile, tile), 1)
    diagonal = diag_ref[pl.ds(front_of(meta_ref[0]), 1), :]
    work_ref[...] = (pivot + pivot.T) * 0.5 + jnp.where(rows == columns, diagonal, 0.0)
    invert(work_ref)
    out_ref[...] = dot3(work_ref[...], chosen_ref[...], ((1,), (1,))).astype(BF16)


def lower_front(level):
    return level // 2


def upper_front(level):
    return 4 + level // 4


def pair_place(meta_ref):
    return (meta_ref[0] & 1) * 4 + (meta_ref[1] >> 1)


def no_place(meta_ref):
    return jnp.int32(0)


def solve(front_of, place_of, meta, diagonals, gathered):
    tile = gathered.shape[-1]
    return call(
        functools.partial(solve_kernel, front_of, place_of),
        jax.ShapeDtypeStruct((tile, tile), BF16),
        [SMEM, VMEM, VMEM],
        VMEM,
        [pltpu.VMEM((tile, tile), F32), pltpu.VMEM((tile, tile), F32)],
        flops=2**29,
        moved=2**22,
    )(meta, diagonals, gathered)


def pivot_slot_of(slots_ref, front):
    slot = jnp.int32(0)
    for index in range(8):
        slot = jnp.where(slots_ref[front, index] == 0, index, slot)
    return slot


def lower_kernel(
    meta_ref, slots_ref, place_ref, chunks_ref, pivot_ref, solved_ref, keep_ref, send_ref, spread_ref, total_ref, update_ref
):
    level, row, col = meta_ref[0], meta_ref[1], meta_ref[2]
    total_ref[...] = jnp.zeros_like(total_ref)
    half = chunks_ref.shape[0] // 2
    for child in range(2):
        dropped = pivot_slot_of(slots_ref, level // 4 * 2 + child) == col
        pivot = pivot_ref[child * half : (child + 1) * half]
        update = jnp.dot(
            pivot.reshape(-1, pivot.shape[-1]), solved_ref[child], preferred_element_type=F32
        )
        update_ref[...] = update.reshape(update_ref.shape)

        def one(index, carry):
            place = jnp.where(dropped, 128, place_ref[child * half + index])
            value = chunks_ref[child * half + index].astype(F32) - update_ref[index]
            total_ref[place] = total_ref[place] + value
            return carry

        lax.fori_loop(0, half, one, 0, unroll=4)
    keep_ref[...] = total_ref[:64]
    send_ref[...] = total_ref[64:128].astype(BF16)
    first = row % 2 * 64
    length, tile = total_ref.shape[1], total_ref.shape[2]
    for column in range(8):
        for part in range(2):
            value = total_ref[part * 64 + column * 8 : part * 64 + column * 8 + 8]
            spread_ref[column, part * 8 * length : (part + 1) * 8 * length] = value.astype(
                BF16
            ).reshape(8 * length, tile)
        panel_tile = first + 8 * slots_ref[4 + level // 4, column]
        spread_ref[column, 16 * length : 17 * length] = total_ref[first].astype(BF16)
        spread_ref[column, 17 * length : 18 * length] = total_ref[panel_tile].astype(BF16)


def upper_kernel(meta_ref, slots_ref, keep_ref, ups_ref, downs_ref, pivot_ref, solved_ref, out_ref):
    level, row, col = meta_ref[0], meta_ref[1], meta_ref[2]
    tile = keep_ref.shape[1]
    dropped = pivot_slot_of(slots_ref, 4 + level // 4) == col
    update = jnp.dot(pivot_ref[...], solved_ref[...], preferred_element_type=F32)
    sent = jnp.concatenate([ups_ref[...], downs_ref[...]], axis=0)
    front = keep_ref[...] + sent.astype(F32)
    result = jnp.where(dropped, 0.0, front - update)
    top = jnp.logical_and(
        lax.broadcasted_iota(jnp.int32, result.shape, 0) < tile // 16, row % 2 == 0
    )
    result = jnp.where(top, 0.0, result).astype(BF16)
    out_ref[...] = result.reshape(out_ref.shape)


def lane_groups(levels):
    groups = []
    for first in range(0, 8, levels):
        for half in range(2):
            groups.append(
                [
                    (first + level) * 8 + 2 * across + half
                    for level in range(levels)
                    for across in range(4)
                ]
            )
    return groups


def exchange(value, levels):
    return lax.all_to_all(
        value,
        ("level", "row"),
        split_axis=0,
        concat_axis=0,
        axis_index_groups=lane_groups(levels),
        tiled=True,
    )


def over_columns(value):
    return lax.all_to_all(value, "col", split_axis=0, concat_axis=0, tiled=True)


def swapped(value, axis, mask):
    return lax.ppermute(value, axis, [(index, index ^ mask) for index in range(8)])


def hopped(value, way):
    pairs = []
    for level in range(8):
        target = (level + 4) % 8
        turn = int(level >= 4) if way > 0 else int(level < 4)
        pairs += [(level * 8 + row, target * 8 + (row ^ turn)) for row in range(8)]
    return lax.ppermute(value, ("level", "row"), pairs)


def tied(*values):
    return lax.optimization_barrier(values)


def picked(pieces, slot):
    return lax.dynamic_index_in_dim(pieces, slot, 0, keepdims=False)


def repeated(value, count):
    return jnp.broadcast_to(value[None], (count,) + value.shape)


def body(leaf_blocks, leaf_tiles, leaf_maps, upper_maps, front_slots, pivot_diag):
    tile = leaf_blocks.shape[2]
    level = lax.axis_index("level")
    row = lax.axis_index("row")
    col = lax.axis_index("col")
    meta = jnp.stack([level, row, col]).astype(jnp.int32)
    positions = jnp.arange(8, dtype=jnp.int32)
    slots = jnp.sum(jnp.where(front_slots == 0, positions[None, :], 0), axis=1)
    eighth, sixteenth = tile // 8, tile // 16
    own = leaf_blocks.reshape(12, tile, tile)

    shares = call(
        share_kernel,
        jax.ShapeDtypeStruct((8, 8, eighth, tile), BF16),
        [SMEM] * 3 + [VMEM],
        VMEM,
        moved=2**21,
    )(meta, leaf_tiles, leaf_maps, own)
    shares = exchange(shares, 2)
    chunks = jnp.swapaxes(own.reshape(12, 16, sixteenth, tile), 0, 1)
    chunks, shares = tied(chunks, shares)
    chunks = exchange(chunks, 4).reshape(8, -1, tile)
    place = call(
        plan_kernel,
        jax.ShapeDtypeStruct((192,), jnp.int32),
        [SMEM] * 4,
        SMEM,
    )(meta, leaf_tiles, leaf_maps, upper_maps)

    shares = call(
        combine_kernel,
        jax.ShapeDtypeStruct((8, eighth, tile), BF16),
        [VMEM],
        VMEM,
        moved=2**21,
    )(shares)
    away = col ^ picked(slots, level // 2)
    for mask in (1, 2, 4):
        shares = jnp.where(away & mask == 0, shares, swapped(shares, "col", mask))
    my_tile = lax.dynamic_slice(front_slots, (level // 2, col), (1, 1))[0, 0]
    parts = jnp.stack([shares[0], picked(shares, my_tile)])
    parts = (parts.astype(F32) + swapped(parts, "row", 1).astype(F32)).astype(BF16)

    chunks, parts = tied(chunks, parts)
    pieces = over_columns(chunks)
    gathered = parts[None]
    for axis, mask in (("row", 2), ("row", 4), ("level", 1)):
        gathered = jnp.concatenate([gathered, swapped(gathered, axis, mask)], axis=0)
    piece = picked(pieces, picked(slots, level // 4 * 2 + col // 4))
    piece, gathered = tied(piece, gathered)
    pivot_columns = over_columns(repeated(piece, 8)).reshape(192, sixteenth, tile)
    solved = solve(lower_front, pair_place, meta, pivot_diag, gathered)
    other = swapped(solved, "level", 2)
    first_child = level // 2 % 2 == 0
    solved = jnp.where(first_child, jnp.stack([solved, other]), jnp.stack([other, solved]))
    keep, send, spread = call(
        lower_kernel,
        (
            jax.ShapeDtypeStruct((64, sixteenth, tile), F32),
            jax.ShapeDtypeStruct((64, sixteenth, tile), BF16),
            jax.ShapeDtypeStruct((8, 18 * sixteenth, tile), BF16),
        ),
        [SMEM, SMEM, SMEM, VMEM, VMEM, VMEM],
        None,
        [pltpu.VMEM((129, sixteenth, tile), F32), pltpu.VMEM((96, sixteenth, tile), F32)],
        flops=2**29,
        moved=2**23,
    )(meta, front_slots, place, chunks.reshape(192, sixteenth, tile), pivot_columns, solved)

    ups, downs = hopped(send[:32], 1), hopped(send[32:], -1)
    spread = picked(over_columns(spread), picked(slots, 4 + level // 4))
    spread, ups, downs = tied(spread, ups, downs)
    spread = spread.astype(F32)
    passed = swapped(spread[8 * sixteenth :].astype(BF16), "row", 1).astype(F32)
    piece = (spread[: 8 * sixteenth] + passed[: 8 * sixteenth]).astype(BF16)
    parts = (spread[16 * sixteenth :] + passed[8 * sixteenth :]).astype(BF16)
    gathered = exchange(repeated(parts.reshape(2, sixteenth, tile), 16), 4)
    piece, gathered = tied(piece, gathered)
    pivot_columns = over_columns(repeated(piece, 8)).reshape(-1, tile)
    solved = solve(upper_front, no_place, meta, pivot_diag, gathered)
    ups, downs = hopped(ups, 1), hopped(downs, -1)
    finished = call(
        upper_kernel,
        jax.ShapeDtypeStruct((16, 4, sixteenth, tile), BF16),
        [SMEM, SMEM, VMEM, VMEM, VMEM, VMEM, VMEM],
        VMEM,
        flops=2**28,
        moved=2**22,
    )(
        meta,
        front_slots,
        keep.reshape(-1, tile),
        ups.reshape(-1, tile),
        downs.reshape(-1, tile),
        pivot_columns,
        solved,
    )
    result = exchange(finished, 4)
    return jnp.swapaxes(result, 0, 1).reshape(1, -1, tile)


def solution(mesh):
    return jax.shard_map(
        body,
        mesh=mesh,
        in_specs=(P("level", "row", "col"), P(), P(), P(), P(), P()),
        out_specs=P("level", "row", "col"),
        check_vma=False,
    )
```

```python
import functools

import jax
import jax.numpy as jnp
from jax import lax
from jax.experimental import pallas as pl
from jax.experimental.pallas import tpu as pltpu
from jax.sharding import PartitionSpec as P

TILE = 256
NPT = 128
STEP = 32
GROUP = 128
AHEAD = 3
HIGHEST = lax.Precision.HIGHEST
VMEM = pltpu.VMEM
SMEM = pltpu.SMEM
INTERPRET = False
F32 = jnp.float32
BF16 = jnp.bfloat16


def call(kernel, out_shape, in_spaces, out_space=None, scratch=(), flops=0, moved=0):
    return pl.pallas_call(
        kernel,
        out_shape=out_shape,
        in_specs=[pl.BlockSpec(memory_space=space) for space in in_spaces],
        out_specs=pl.BlockSpec(memory_space=out_space)
        if out_space is not None
        else [pl.BlockSpec(memory_space=VMEM) for _ in out_shape],
        scratch_shapes=list(scratch),
        compiler_params=pltpu.CompilerParams(vmem_limit_bytes=32 * 2**20),
        cost_estimate=pl.CostEstimate(flops=flops, bytes_accessed=moved, transcendentals=0),
        interpret=INTERPRET,
    )


def plan_kernel(meta_ref, tiles_ref, leaf_maps_ref, upper_maps_ref, place_ref):
    half = meta_ref[1] & 1
    base = meta_ref[0] & 4
    for source in range(16):
        leaf = base + source // 4
        front = (base >> 1) + source // 8
        live = tiles_ref[leaf]
        first = (2 * (source % 4) + half) * 12
        for tile in range(12):
            lower_tile = leaf_maps_ref[leaf, first + tile]
            upper_tile = upper_maps_ref[front, lower_tile]
            home_row = (upper_tile >> 2) & 7
            position = ((upper_tile >> 5) << 4) + ((home_row >> 1) << 2) + (upper_tile & 3)
            position = position + ((home_row & 1) << 6)
            kept = jnp.logical_and(first + tile < live, lower_tile != 0)
            place_ref[source * 12 + tile] = jnp.where(kept, position, 128)


def share_kernel(meta_ref, tiles_ref, leaf_maps_ref, leaf_ref, out_ref):
    level, row = meta_ref[0], meta_ref[1]
    tile = leaf_ref.shape[1]
    across, rows = out_ref.shape[0], out_ref.shape[2]
    out_ref[...] = jnp.zeros_like(out_ref)

    def look(index, carry):
        leaf_tile = row * 12 + index
        lower_tile = leaf_maps_ref[level, leaf_tile]
        match = jnp.logical_and(lower_tile % 16 == 0, leaf_tile < tiles_ref[level])

        @pl.when(match)
        def _():
            out_ref[:, lower_tile // 16] = leaf_ref[index].reshape(across, rows, tile)

        return carry

    lax.fori_loop(0, 12, look, 0)


def combine_kernel(shares_ref, out_ref):
    total = shares_ref[0].astype(F32)
    for source in range(1, shares_ref.shape[0]):
        total = total + shares_ref[source].astype(F32)
    out_ref[...] = total.astype(BF16)


def split(value):
    high = value.astype(BF16).astype(F32)
    return high, value - high


def dot3(left, right, dims):
    left_high, left_low = (part.astype(BF16) for part in split(left))
    right_high, right_low = (part.astype(BF16) for part in split(right))
    product = functools.partial(
        lax.dot_general, dimension_numbers=(dims, ((), ())), preferred_element_type=F32
    )
    return (product(left_low, right_high) + product(left_high, right_low)) + product(
        left_high, right_high
    )


def invert(work_ref):
    tile = work_ref.shape[0]
    group = min(GROUP, tile)
    groups = tile // group
    ids = lax.broadcasted_iota(jnp.int32, (STEP, group), 0)
    lanes = lax.broadcasted_iota(jnp.int32, (1, group), 1)
    for start in range(0, tile, STEP):
        own = start // group
        offset = start - own * group
        rows = slice(start, start + STEP)
        block = [work_ref[rows, k * group : (k + 1) * group] for k in range(groups)]

        def column(step):
            lane = offset + step
            return jnp.broadcast_to(block[own][:, lane : lane + 1], (STEP, group))

        ahead = [column(step) for step in range(AHEAD)]
        for step in range(STEP):
            if step + AHEAD < STEP:
                ahead.append(column(step + AHEAD))
            here = ahead.pop(0)
            inverse = 1.0 / here[step : step + 1]
            pivot_row = ids == step
            pivot_lane = lanes == offset + step
            for k in range(len(ahead)):
                scaled = ahead[k][step : step + 1] * inverse
                ahead[k] = jnp.where(pivot_row, scaled, ahead[k] - here * scaled)
            for k in range(groups):
                value = block[k]
                scaled = value[step : step + 1]
                if k == own:
                    scaled = jnp.where(pivot_lane, 1.0, scaled)
                    value = jnp.where(pivot_lane, 0.0, value)
                scaled = scaled * inverse
                block[k] = jnp.where(pivot_row, scaled, value - here * scaled)
        factor = work_ref[:, own * group : (own + 1) * group]
        fac_rows = lax.broadcasted_iota(jnp.int32, factor.shape, 0)
        fac_cols = lax.broadcasted_iota(jnp.int32, factor.shape, 1)
        own_row = jnp.logical_and(fac_rows >= start, fac_rows < start + STEP)
        own_col = jnp.logical_and(fac_cols >= offset, fac_cols < offset + STEP)
        work_ref[:, own * group : (own + 1) * group] = jnp.where(own_col, 0.0, factor)
        factor = jnp.where(jnp.logical_and(own_col, jnp.logical_not(own_row)), factor, 0.0)
        whole = jnp.concatenate(block, axis=1)
        if group >= 4 * STEP:
            high, low = split(factor)
            factor = high + pltpu.roll(high, STEP, 1) + pltpu.roll(low, 2 * STEP, 1)
            whole_high, whole_low = (part.astype(BF16) for part in split(whole))
            pieces = [jnp.zeros((STEP, tile), BF16) for _ in range(group // STEP)]
            place = offset // STEP
            for shift, part in enumerate((whole_high, whole_low, whole_high)):
                pieces[(place + shift) % len(pieces)] = part
            update = jnp.dot(
                factor.astype(BF16), jnp.concatenate(pieces, axis=0), preferred_element_type=F32
            )
        else:
            update = jnp.dot(
                factor[:, offset : offset + STEP], whole, precision=HIGHEST, preferred_element_type=F32
            )
        work_ref[...] = work_ref[...] - update
        work_ref[rows, :] = whole


def solve_kernel(front_of, place_of, meta_ref, diag_ref, gathered_ref, out_ref, work_ref, chosen_ref):
    tile = out_ref.shape[0]
    count, length = gathered_ref.shape[0], gathered_ref.shape[2]
    place = place_of(meta_ref)
    for piece in range(count):
        rows = pl.ds(pl.multiple_of((place ^ piece) * length, length), length)
        work_ref[rows, :] = gathered_ref[piece, 0].astype(F32)
        chosen_ref[rows, :] = gathered_ref[piece, 1].astype(F32)
    pivot = work_ref[...]
    rows = lax.broadcasted_iota(jnp.int32, (tile, tile), 0)
    columns = lax.broadcasted_iota(jnp.int32, (tile, tile), 1)
    diagonal = diag_ref[pl.ds(front_of(meta_ref[0]), 1), :]
    work_ref[...] = (pivot + pivot.T) * 0.5 + jnp.where(rows == columns, diagonal, 0.0)
    invert(work_ref)
    out_ref[...] = dot3(work_ref[...], chosen_ref[...], ((1,), (1,))).astype(BF16)


def lower_front(level):
    return level // 2


def upper_front(level):
    return 4 + level // 4


def pair_place(meta_ref):
    return (meta_ref[0] & 1) * 4 + (meta_ref[1] >> 1)


def quad_place(meta_ref):
    return (meta_ref[0] & 3) * 4 + (meta_ref[1] >> 1)


def solve(front_of, place_of, meta, diagonals, gathered):
    tile = gathered.shape[-1]
    return call(
        functools.partial(solve_kernel, front_of, place_of),
        jax.ShapeDtypeStruct((tile, tile), BF16),
        [SMEM, VMEM, VMEM],
        VMEM,
        [pltpu.VMEM((tile, tile), F32), pltpu.VMEM((tile, tile), F32)],
        flops=2**29,
        moved=2**22,
    )(meta, diagonals, gathered)


def pivot_slot_of(slots_ref, front):
    slot = jnp.int32(0)
    for index in range(8):
        slot = jnp.where(slots_ref[front, index] == 0, index, slot)
    return slot


def lower_kernel(
    meta_ref, slots_ref, place_ref, chunks_ref, pivot_ref, solved_ref, halves_ref, share_ref, total_ref, update_ref
):
    level, col = meta_ref[0], meta_ref[2]
    total_ref[...] = jnp.zeros_like(total_ref)
    half = chunks_ref.shape[0] // 2
    for child in range(2):
        dropped = pivot_slot_of(slots_ref, level // 4 * 2 + child) == col
        pivot = pivot_ref[child * half : (child + 1) * half]
        update = jnp.dot(
            pivot.reshape(-1, pivot.shape[-1]), solved_ref[child], preferred_element_type=F32
        )
        update_ref[...] = update.reshape(update_ref.shape)

        def one(index, carry):
            place = jnp.where(dropped, 128, place_ref[child * half + index])
            value = chunks_ref[child * half + index].astype(F32) - update_ref[index]
            total_ref[place] = total_ref[place] + value
            return carry

        lax.fori_loop(0, half, one, 0, unroll=4)
    halves_ref[0] = total_ref[:64].astype(BF16)
    halves_ref[1] = total_ref[64:128].astype(BF16)
    for tile in range(8):
        share_ref[tile] = total_ref[8 * tile].astype(BF16)


def upper_kernel(meta_ref, slots_ref, halves_ref, pivot_ref, solved_ref, out_ref):
    level, row, col = meta_ref[0], meta_ref[1], meta_ref[2]
    tile = halves_ref.shape[2]
    dropped = pivot_slot_of(slots_ref, 4 + level // 4) == col
    update = jnp.dot(pivot_ref[...], solved_ref[...], preferred_element_type=F32)
    front = halves_ref[0].astype(F32) + halves_ref[1].astype(F32)
    result = jnp.where(dropped, 0.0, front - update)
    top = jnp.logical_and(
        lax.broadcasted_iota(jnp.int32, result.shape, 0) < tile // 16, row % 2 == 0
    )
    result = jnp.where(top, 0.0, result).astype(BF16)
    out_ref[...] = result.reshape(out_ref.shape)


def lane_groups(levels):
    groups = []
    for first in range(0, 8, levels):
        for half in range(2):
            groups.append(
                [
                    (first + level) * 8 + 2 * across + half
                    for level in range(levels)
                    for across in range(4)
                ]
            )
    return groups


def exchange(value, levels):
    return lax.all_to_all(
        value,
        ("level", "row"),
        split_axis=0,
        concat_axis=0,
        axis_index_groups=lane_groups(levels),
        tiled=True,
    )


def over_columns(value):
    return lax.all_to_all(value, "col", split_axis=0, concat_axis=0, tiled=True)


def swapped(value, axis, mask):
    return lax.ppermute(value, axis, [(index, index ^ mask) for index in range(8)])


def tied(first, second):
    return lax.optimization_barrier((first, second))


def picked(pieces, slot):
    return lax.dynamic_index_in_dim(pieces, slot, 0, keepdims=False)


def repeated(value, count):
    return jnp.broadcast_to(value[None], (count,) + value.shape)


def own_parts(shares, away, my_tile):
    for mask in (1, 2, 4):
        shares = jnp.where(away & mask == 0, shares, swapped(shares, "col", mask))
    parts = jnp.stack([shares[0], picked(shares, my_tile)])
    return (parts.astype(F32) + swapped(parts, "row", 1).astype(F32)).astype(BF16)


def doubled(parts, steps):
    gathered = parts[None]
    for axis, mask in steps:
        gathered = jnp.concatenate([gathered, swapped(gathered, axis, mask)], axis=0)
    return gathered


def body(leaf_blocks, leaf_tiles, leaf_maps, upper_maps, front_slots, pivot_diag):
    tile = leaf_blocks.shape[2]
    level = lax.axis_index("level")
    row = lax.axis_index("row")
    col = lax.axis_index("col")
    meta = jnp.stack([level, row, col]).astype(jnp.int32)
    positions = jnp.arange(8, dtype=jnp.int32)
    slots = jnp.sum(jnp.where(front_slots == 0, positions[None, :], 0), axis=1)
    eighth, sixteenth = tile // 8, tile // 16
    own = leaf_blocks.reshape(12, tile, tile)

    shares = call(
        share_kernel,
        jax.ShapeDtypeStruct((8, 8, eighth, tile), BF16),
        [SMEM] * 3 + [VMEM],
        VMEM,
        moved=2**21,
    )(meta, leaf_tiles, leaf_maps, own)
    shares = exchange(shares, 2)
    chunks = jnp.swapaxes(own.reshape(12, 16, sixteenth, tile), 0, 1)
    chunks, shares = tied(chunks, shares)
    chunks = exchange(chunks, 4).reshape(8, -1, tile)
    place = call(
        plan_kernel,
        jax.ShapeDtypeStruct((192,), jnp.int32),
        [SMEM] * 4,
        SMEM,
    )(meta, leaf_tiles, leaf_maps, upper_maps)

    shares = call(
        combine_kernel,
        jax.ShapeDtypeStruct((8, eighth, tile), BF16),
        [VMEM],
        VMEM,
        moved=2**21,
    )(shares)
    front = level // 2
    my_tile = lax.dynamic_slice(front_slots, (front, col), (1, 1))[0, 0]
    parts = own_parts(shares, col ^ picked(slots, front), my_tile)
    chunks, parts = tied(chunks, parts)
    pieces = over_columns(chunks)
    gathered = doubled(parts, (("row", 2), ("row", 4), ("level", 1)))
    piece = picked(pieces, picked(slots, level // 4 * 2 + col // 4))
    piece, gathered = tied(piece, gathered)
    pivot_columns = over_columns(repeated(piece, 8)).reshape(192, sixteenth, tile)
    solved = solve(lower_front, pair_place, meta, pivot_diag, gathered)
    other = swapped(solved, "level", 2)
    first_child = level // 2 % 2 == 0
    solved = jnp.where(first_child, jnp.stack([solved, other]), jnp.stack([other, solved]))
    halves, shares = call(
        lower_kernel,
        (
            jax.ShapeDtypeStruct((2, 64, sixteenth, tile), BF16),
            jax.ShapeDtypeStruct((8, sixteenth, tile), BF16),
        ),
        [SMEM, SMEM, SMEM, VMEM, VMEM, VMEM],
        None,
        [pltpu.VMEM((129, sixteenth, tile), F32), pltpu.VMEM((96, sixteenth, tile), F32)],
        flops=2**29,
        moved=2**23,
    )(meta, front_slots, place, chunks.reshape(192, sixteenth, tile), pivot_columns, solved)

    halves = lax.all_to_all(
        halves.reshape(2, -1, tile),
        "row",
        split_axis=0,
        concat_axis=0,
        axis_index_groups=[[0, 1], [2, 3], [4, 5], [6, 7]],
        tiled=True,
    )
    front = 4 + level // 4
    my_tile = lax.dynamic_slice(front_slots, (front, col), (1, 1))[0, 0]
    upper_slot = picked(slots, front)
    parts = own_parts(shares, col ^ upper_slot, my_tile)
    halves, parts = tied(halves, parts)
    rounded = (halves[0].astype(F32) + halves[1].astype(F32)).astype(BF16)
    piece = picked(over_columns(rounded.reshape(8, -1, tile)), upper_slot)
    gathered = doubled(parts, (("row", 2), ("row", 4), ("level", 1), ("level", 2)))
    piece, gathered = tied(piece, gathered)
    pivot_columns = over_columns(repeated(piece, 8)).reshape(-1, tile)
    solved = solve(upper_front, quad_place, meta, pivot_diag, gathered)
    finished = call(
        upper_kernel,
        jax.ShapeDtypeStruct((16, 4, sixteenth, tile), BF16),
        [SMEM, SMEM, VMEM, VMEM, VMEM],
        VMEM,
        flops=2**28,
        moved=2**22,
    )(meta, front_slots, halves, pivot_columns, solved)
    result = exchange(finished, 4)
    return jnp.swapaxes(result, 0, 1).reshape(1, -1, tile)


def solution(mesh):
    return jax.shard_map(
        body,
        mesh=mesh,
        in_specs=(P("level", "row", "col"), P(), P(), P(), P(), P()),
        out_specs=P("level", "row", "col"),
        check_vma=False,
    )
```

```python
import functools

import jax
import jax.numpy as jnp
from jax import lax
from jax.experimental import pallas as pl
from jax.experimental.pallas import tpu as pltpu
from jax.sharding import PartitionSpec as P

TILE = 256
NPT = 128
STEP = 32
GROUP = 128
AHEAD = 3
HIGHEST = lax.Precision.HIGHEST
VMEM = pltpu.VMEM
SMEM = pltpu.SMEM
INTERPRET = False
F32 = jnp.float32
BF16 = jnp.bfloat16


def call(kernel, out_shape, in_spaces, out_space=None, scratch=(), flops=0, moved=0):
    return pl.pallas_call(
        kernel,
        out_shape=out_shape,
        in_specs=[pl.BlockSpec(memory_space=space) for space in in_spaces],
        out_specs=pl.BlockSpec(memory_space=out_space)
        if out_space is not None
        else [pl.BlockSpec(memory_space=VMEM) for _ in out_shape],
        scratch_shapes=list(scratch),
        compiler_params=pltpu.CompilerParams(vmem_limit_bytes=32 * 2**20),
        cost_estimate=pl.CostEstimate(flops=flops, bytes_accessed=moved, transcendentals=0),
        interpret=INTERPRET,
    )


def plan_kernel(meta_ref, tiles_ref, leaf_maps_ref, upper_maps_ref, place_ref):
    half = meta_ref[1] & 1
    base = meta_ref[0] & 4
    for source in range(16):
        leaf = base + source // 4
        front = (base >> 1) + source // 8
        live = tiles_ref[leaf]
        first = (2 * (source % 4) + half) * 12
        for tile in range(12):
            lower_tile = leaf_maps_ref[leaf, first + tile]
            upper_tile = upper_maps_ref[front, lower_tile]
            home_row = (upper_tile >> 2) & 7
            position = ((upper_tile >> 5) << 4) + ((home_row >> 1) << 2) + (upper_tile & 3)
            position = position + (((home_row & 1) ^ half) << 6)
            kept = jnp.logical_and(first + tile < live, lower_tile != 0)
            place_ref[source * 12 + tile] = jnp.where(kept, position, 128)


def share_kernel(meta_ref, tiles_ref, leaf_maps_ref, leaf_ref, out_ref):
    level, row = meta_ref[0], meta_ref[1]
    tile = leaf_ref.shape[1]
    across, rows = out_ref.shape[0], out_ref.shape[2]
    out_ref[...] = jnp.zeros_like(out_ref)

    def look(index, carry):
        leaf_tile = row * 12 + index
        lower_tile = leaf_maps_ref[level, leaf_tile]
        match = jnp.logical_and(lower_tile % 16 == 0, leaf_tile < tiles_ref[level])

        @pl.when(match)
        def _():
            out_ref[:, lower_tile // 16] = leaf_ref[index].reshape(across, rows, tile)

        return carry

    lax.fori_loop(0, 12, look, 0)


def combine_kernel(shares_ref, out_ref):
    total = shares_ref[0].astype(F32)
    for source in range(1, shares_ref.shape[0]):
        total = total + shares_ref[source].astype(F32)
    out_ref[...] = total.astype(BF16)


def split(value):
    high = value.astype(BF16).astype(F32)
    return high, value - high


def dot3(left, right, dims):
    left_high, left_low = (part.astype(BF16) for part in split(left))
    right_high, right_low = (part.astype(BF16) for part in split(right))
    product = functools.partial(
        lax.dot_general, dimension_numbers=(dims, ((), ())), preferred_element_type=F32
    )
    return (product(left_low, right_high) + product(left_high, right_low)) + product(
        left_high, right_high
    )


def invert(work_ref):
    tile = work_ref.shape[0]
    group = min(GROUP, tile)
    groups = tile // group
    ids = lax.broadcasted_iota(jnp.int32, (STEP, group), 0)
    lanes = lax.broadcasted_iota(jnp.int32, (1, group), 1)
    for start in range(0, tile, STEP):
        own = start // group
        offset = start - own * group
        rows = slice(start, start + STEP)
        block = [work_ref[rows, k * group : (k + 1) * group] for k in range(groups)]

        def column(step):
            lane = offset + step
            return jnp.broadcast_to(block[own][:, lane : lane + 1], (STEP, group))

        ahead = [column(step) for step in range(AHEAD)]
        for step in range(STEP):
            if step + AHEAD < STEP:
                ahead.append(column(step + AHEAD))
            here = ahead.pop(0)
            inverse = 1.0 / here[step : step + 1]
            pivot_row = ids == step
            pivot_lane = lanes == offset + step
            for k in range(len(ahead)):
                scaled = ahead[k][step : step + 1] * inverse
                ahead[k] = jnp.where(pivot_row, scaled, ahead[k] - here * scaled)
            for k in range(groups):
                value = block[k]
                scaled = value[step : step + 1]
                if k == own:
                    scaled = jnp.where(pivot_lane, 1.0, scaled)
                    value = jnp.where(pivot_lane, 0.0, value)
                scaled = scaled * inverse
                block[k] = jnp.where(pivot_row, scaled, value - here * scaled)
        factor = work_ref[:, own * group : (own + 1) * group]
        fac_rows = lax.broadcasted_iota(jnp.int32, factor.shape, 0)
        fac_cols = lax.broadcasted_iota(jnp.int32, factor.shape, 1)
        own_row = jnp.logical_and(fac_rows >= start, fac_rows < start + STEP)
        own_col = jnp.logical_and(fac_cols >= offset, fac_cols < offset + STEP)
        work_ref[:, own * group : (own + 1) * group] = jnp.where(own_col, 0.0, factor)
        factor = jnp.where(jnp.logical_and(own_col, jnp.logical_not(own_row)), factor, 0.0)
        whole = jnp.concatenate(block, axis=1)
        if group >= 4 * STEP:
            high, low = split(factor)
            factor = high + pltpu.roll(high, STEP, 1) + pltpu.roll(low, 2 * STEP, 1)
            whole_high, whole_low = (part.astype(BF16) for part in split(whole))
            pieces = [jnp.zeros((STEP, tile), BF16) for _ in range(group // STEP)]
            place = offset // STEP
            for shift, part in enumerate((whole_high, whole_low, whole_high)):
                pieces[(place + shift) % len(pieces)] = part
            update = jnp.dot(
                factor.astype(BF16), jnp.concatenate(pieces, axis=0), preferred_element_type=F32
            )
        else:
            update = jnp.dot(
                factor[:, offset : offset + STEP], whole, precision=HIGHEST, preferred_element_type=F32
            )
        work_ref[...] = work_ref[...] - update
        work_ref[rows, :] = whole


def solve_kernel(front_of, place_of, meta_ref, diag_ref, gathered_ref, out_ref, work_ref, chosen_ref):
    tile = out_ref.shape[0]
    count, length = gathered_ref.shape[0], gathered_ref.shape[2]
    place = place_of(meta_ref)
    for piece in range(count):
        rows = pl.ds(pl.multiple_of((place ^ piece) * length, length), length)
        work_ref[rows, :] = gathered_ref[piece, 0].astype(F32)
        chosen_ref[rows, :] = gathered_ref[piece, 1].astype(F32)
    pivot = work_ref[...]
    rows = lax.broadcasted_iota(jnp.int32, (tile, tile), 0)
    columns = lax.broadcasted_iota(jnp.int32, (tile, tile), 1)
    diagonal = diag_ref[pl.ds(front_of(meta_ref[0]), 1), :]
    work_ref[...] = (pivot + pivot.T) * 0.5 + jnp.where(rows == columns, diagonal, 0.0)
    invert(work_ref)
    out_ref[...] = dot3(work_ref[...], chosen_ref[...], ((1,), (1,))).astype(BF16)


def lower_front(level):
    return level // 2


def upper_front(level):
    return 4 + level // 4


def pair_place(meta_ref):
    return (meta_ref[0] & 1) * 4 + (meta_ref[1] >> 1)


def no_place(meta_ref):
    return jnp.int32(0)


def solve(front_of, place_of, meta, diagonals, gathered):
    tile = gathered.shape[-1]
    return call(
        functools.partial(solve_kernel, front_of, place_of),
        jax.ShapeDtypeStruct((tile, tile), BF16),
        [SMEM, VMEM, VMEM],
        VMEM,
        [pltpu.VMEM((tile, tile), F32), pltpu.VMEM((tile, tile), F32)],
        flops=2**29,
        moved=2**22,
    )(meta, diagonals, gathered)


def pivot_slot_of(slots_ref, front):
    slot = jnp.int32(0)
    for index in range(8):
        slot = jnp.where(slots_ref[front, index] == 0, index, slot)
    return slot


def lower_kernel(
    meta_ref, slots_ref, place_ref, chunks_ref, pivot_ref, solved_ref, keep_ref, send_ref, spread_ref, total_ref, update_ref
):
    level, row, col = meta_ref[0], meta_ref[1], meta_ref[2]
    total_ref[...] = jnp.zeros_like(total_ref)
    half = chunks_ref.shape[0] // 2
    for child in range(2):
        dropped = pivot_slot_of(slots_ref, level // 4 * 2 + child) == col
        pivot = pivot_ref[child * half : (child + 1) * half]
        update = jnp.dot(
            pivot.reshape(-1, pivot.shape[-1]), solved_ref[child], preferred_element_type=F32
        )
        update_ref[...] = update.reshape(update_ref.shape)

        def one(index, carry):
            place = jnp.where(dropped, 128, place_ref[child * half + index])
            value = chunks_ref[child * half + index].astype(F32) - update_ref[index]
            total_ref[place] = total_ref[place] + value
            return carry

        lax.fori_loop(0, half, one, 0, unroll=4)
    keep_ref[...] = total_ref[:64]
    send_ref[...] = total_ref[64:128].astype(BF16)
    first = row % 2 * 64
    length, tile = total_ref.shape[1], total_ref.shape[2]
    for column in range(8):
        for part in range(2):
            value = total_ref[part * 64 + column * 8 : part * 64 + column * 8 + 8]
            spread_ref[column, part * 8 * length : (part + 1) * 8 * length] = value.astype(
                BF16
            ).reshape(8 * length, tile)
        panel_tile = first + 8 * slots_ref[4 + level // 4, column]
        spread_ref[column, 16 * length : 17 * length] = total_ref[first].astype(BF16)
        spread_ref[column, 17 * length : 18 * length] = total_ref[panel_tile].astype(BF16)


def upper_kernel(meta_ref, slots_ref, keep_ref, sent_ref, pivot_ref, solved_ref, out_ref):
    level, row, col = meta_ref[0], meta_ref[1], meta_ref[2]
    tile = keep_ref.shape[1]
    dropped = pivot_slot_of(slots_ref, 4 + level // 4) == col
    update = jnp.dot(pivot_ref[...], solved_ref[...], preferred_element_type=F32)
    front = keep_ref[...] + sent_ref[...].astype(F32)
    result = jnp.where(dropped, 0.0, front - update)
    top = jnp.logical_and(
        lax.broadcasted_iota(jnp.int32, result.shape, 0) < tile // 16, row % 2 == 0
    )
    result = jnp.where(top, 0.0, result).astype(BF16)
    out_ref[...] = result.reshape(out_ref.shape)


def lane_groups(levels):
    groups = []
    for first in range(0, 8, levels):
        for half in range(2):
            groups.append(
                [
                    (first + level) * 8 + 2 * across + half
                    for level in range(levels)
                    for across in range(4)
                ]
            )
    return groups


def exchange(value, levels):
    return lax.all_to_all(
        value,
        ("level", "row"),
        split_axis=0,
        concat_axis=0,
        axis_index_groups=lane_groups(levels),
        tiled=True,
    )


def over_columns(value):
    return lax.all_to_all(value, "col", split_axis=0, concat_axis=0, tiled=True)


def swapped(value, axis, mask):
    return lax.ppermute(value, axis, [(index, index ^ mask) for index in range(8)])


def tied(*values):
    return lax.optimization_barrier(values)


def picked(pieces, slot):
    return lax.dynamic_index_in_dim(pieces, slot, 0, keepdims=False)


def repeated(value, count):
    return jnp.broadcast_to(value[None], (count,) + value.shape)


def body(leaf_blocks, leaf_tiles, leaf_maps, upper_maps, front_slots, pivot_diag):
    tile = leaf_blocks.shape[2]
    level = lax.axis_index("level")
    row = lax.axis_index("row")
    col = lax.axis_index("col")
    meta = jnp.stack([level, row, col]).astype(jnp.int32)
    positions = jnp.arange(8, dtype=jnp.int32)
    slots = jnp.sum(jnp.where(front_slots == 0, positions[None, :], 0), axis=1)
    eighth, sixteenth = tile // 8, tile // 16
    own = leaf_blocks.reshape(12, tile, tile)

    shares = call(
        share_kernel,
        jax.ShapeDtypeStruct((8, 8, eighth, tile), BF16),
        [SMEM] * 3 + [VMEM],
        VMEM,
        moved=2**21,
    )(meta, leaf_tiles, leaf_maps, own)
    shares = exchange(shares, 2)
    chunks = jnp.swapaxes(own.reshape(12, 16, sixteenth, tile), 0, 1)
    chunks, shares = tied(chunks, shares)
    chunks = exchange(chunks, 4).reshape(8, -1, tile)
    place = call(
        plan_kernel,
        jax.ShapeDtypeStruct((192,), jnp.int32),
        [SMEM] * 4,
        SMEM,
    )(meta, leaf_tiles, leaf_maps, upper_maps)

    shares = call(
        combine_kernel,
        jax.ShapeDtypeStruct((8, eighth, tile), BF16),
        [VMEM],
        VMEM,
        moved=2**21,
    )(shares)
    away = col ^ picked(slots, level // 2)
    for mask in (1, 2, 4):
        shares = jnp.where(away & mask == 0, shares, swapped(shares, "col", mask))
    my_tile = lax.dynamic_slice(front_slots, (level // 2, col), (1, 1))[0, 0]
    parts = jnp.stack([shares[0], picked(shares, my_tile)])
    parts = (parts.astype(F32) + swapped(parts, "row", 1).astype(F32)).astype(BF16)

    chunks, parts = tied(chunks, parts)
    pieces = over_columns(chunks)
    gathered = parts[None]
    for axis, mask in (("row", 2), ("row", 4), ("level", 1)):
        gathered = jnp.concatenate([gathered, swapped(gathered, axis, mask)], axis=0)
    piece = picked(pieces, picked(slots, level // 4 * 2 + col // 4))
    piece, gathered = tied(piece, gathered)
    pivot_columns = over_columns(repeated(piece, 8)).reshape(192, sixteenth, tile)
    solved = solve(lower_front, pair_place, meta, pivot_diag, gathered)
    other = swapped(solved, "level", 2)
    first_child = level // 2 % 2 == 0
    solved = jnp.where(first_child, jnp.stack([solved, other]), jnp.stack([other, solved]))
    keep, send, spread = call(
        lower_kernel,
        (
            jax.ShapeDtypeStruct((64, sixteenth, tile), F32),
            jax.ShapeDtypeStruct((64, sixteenth, tile), BF16),
            jax.ShapeDtypeStruct((8, 18 * sixteenth, tile), BF16),
        ),
        [SMEM, SMEM, SMEM, VMEM, VMEM, VMEM],
        None,
        [pltpu.VMEM((129, sixteenth, tile), F32), pltpu.VMEM((96, sixteenth, tile), F32)],
        flops=2**29,
        moved=2**23,
    )(meta, front_slots, place, chunks.reshape(192, sixteenth, tile), pivot_columns, solved)

    sent = swapped(send, "row", 1)
    spread = picked(over_columns(spread), picked(slots, 4 + level // 4))
    spread, sent = tied(spread, sent)
    spread = spread.astype(F32)
    passed = swapped(spread[8 * sixteenth :].astype(BF16), "row", 1).astype(F32)
    piece = (spread[: 8 * sixteenth] + passed[: 8 * sixteenth]).astype(BF16)
    parts = (spread[16 * sixteenth :] + passed[8 * sixteenth :]).astype(BF16)
    gathered = exchange(repeated(parts.reshape(2, sixteenth, tile), 16), 4)
    piece, gathered = tied(piece, gathered)
    pivot_columns = over_columns(repeated(piece, 8)).reshape(-1, tile)
    solved = solve(upper_front, no_place, meta, pivot_diag, gathered)
    finished = call(
        upper_kernel,
        jax.ShapeDtypeStruct((16, 4, sixteenth, tile), BF16),
        [SMEM, SMEM, VMEM, VMEM, VMEM, VMEM],
        VMEM,
        flops=2**28,
        moved=2**22,
    )(
        meta,
        front_slots,
        keep.reshape(-1, tile),
        sent.reshape(-1, tile),
        pivot_columns,
        solved,
    )
    result = exchange(finished, 4)
    return jnp.swapaxes(result, 0, 1).reshape(1, -1, tile)


def solution(mesh):
    return jax.shard_map(
        body,
        mesh=mesh,
        in_specs=(P("level", "row", "col"), P(), P(), P(), P(), P()),
        out_specs=P("level", "row", "col"),
        check_vma=False,
    )
```

```python
import functools

import jax
import jax.numpy as jnp
from jax import lax
from jax.experimental import pallas as pl
from jax.experimental.pallas import tpu as pltpu
from jax.sharding import PartitionSpec as P

TILE = 256
NPT = 128
STEP = 32
GROUP = 128
AHEAD = 3
HIGHEST = lax.Precision.HIGHEST
VMEM = pltpu.VMEM
SMEM = pltpu.SMEM
INTERPRET = False
F32 = jnp.float32
BF16 = jnp.bfloat16


def call(kernel, out_shape, in_spaces, out_space=None, scratch=(), flops=0, moved=0):
    return pl.pallas_call(
        kernel,
        out_shape=out_shape,
        in_specs=[pl.BlockSpec(memory_space=space) for space in in_spaces],
        out_specs=pl.BlockSpec(memory_space=out_space)
        if out_space is not None
        else [pl.BlockSpec(memory_space=VMEM) for _ in out_shape],
        scratch_shapes=list(scratch),
        compiler_params=pltpu.CompilerParams(vmem_limit_bytes=32 * 2**20),
        cost_estimate=pl.CostEstimate(flops=flops, bytes_accessed=moved, transcendentals=0),
        interpret=INTERPRET,
    )


def plan_kernel(meta_ref, tiles_ref, leaf_maps_ref, upper_maps_ref, place_ref):
    half = meta_ref[1] & 1
    base = meta_ref[0] & 4
    for source in range(16):
        leaf = base + source // 4
        front = (base >> 1) + source // 8
        live = tiles_ref[leaf]
        first = (2 * (source % 4) + half) * 12
        for tile in range(12):
            lower_tile = leaf_maps_ref[leaf, first + tile]
            upper_tile = upper_maps_ref[front, lower_tile]
            home_row = (upper_tile >> 2) & 7
            position = ((upper_tile >> 5) << 4) + ((home_row >> 1) << 2) + (upper_tile & 3)
            position = position + (((home_row & 1) ^ half) << 6)
            kept = jnp.logical_and(first + tile < live, lower_tile != 0)
            place_ref[source * 12 + tile] = jnp.where(kept, position, 128)


def share_kernel(meta_ref, tiles_ref, leaf_maps_ref, leaf_ref, out_ref):
    level, row = meta_ref[0], meta_ref[1]
    tile = leaf_ref.shape[1]
    across, rows = out_ref.shape[0], out_ref.shape[2]
    out_ref[...] = jnp.zeros_like(out_ref)

    def look(index, carry):
        leaf_tile = row * 12 + index
        lower_tile = leaf_maps_ref[level, leaf_tile]
        match = jnp.logical_and(lower_tile % 16 == 0, leaf_tile < tiles_ref[level])

        @pl.when(match)
        def _():
            out_ref[:, lower_tile // 16] = leaf_ref[index].reshape(across, rows, tile)

        return carry

    lax.fori_loop(0, 12, look, 0)


def combine_kernel(shares_ref, out_ref):
    total = shares_ref[0].astype(F32)
    for source in range(1, shares_ref.shape[0]):
        total = total + shares_ref[source].astype(F32)
    out_ref[...] = total.astype(BF16)


def split(value):
    high = value.astype(BF16).astype(F32)
    return high, value - high


def dot3(left, right, dims):
    left_high, left_low = (part.astype(BF16) for part in split(left))
    right_high, right_low = (part.astype(BF16) for part in split(right))
    product = functools.partial(
        lax.dot_general, dimension_numbers=(dims, ((), ())), preferred_element_type=F32
    )
    return (product(left_low, right_high) + product(left_high, right_low)) + product(
        left_high, right_high
    )


def invert(work_ref):
    tile = work_ref.shape[0]
    group = min(GROUP, tile)
    groups = tile // group
    ids = lax.broadcasted_iota(jnp.int32, (STEP, group), 0)
    lanes = lax.broadcasted_iota(jnp.int32, (1, group), 1)
    for start in range(0, tile, STEP):
        own = start // group
        offset = start - own * group
        rows = slice(start, start + STEP)
        block = [work_ref[rows, k * group : (k + 1) * group] for k in range(groups)]

        def column(step):
            lane = offset + step
            return jnp.broadcast_to(block[own][:, lane : lane + 1], (STEP, group))

        ahead = [column(step) for step in range(AHEAD)]
        for step in range(STEP):
            if step + AHEAD < STEP:
                ahead.append(column(step + AHEAD))
            here = ahead.pop(0)
            inverse = 1.0 / here[step : step + 1]
            pivot_row = ids == step
            pivot_lane = lanes == offset + step
            for k in range(len(ahead)):
                scaled = ahead[k][step : step + 1] * inverse
                ahead[k] = jnp.where(pivot_row, scaled, ahead[k] - here * scaled)
            for k in range(groups):
                value = block[k]
                scaled = value[step : step + 1]
                if k == own:
                    scaled = jnp.where(pivot_lane, 1.0, scaled)
                    value = jnp.where(pivot_lane, 0.0, value)
                scaled = scaled * inverse
                block[k] = jnp.where(pivot_row, scaled, value - here * scaled)
        factor = work_ref[:, own * group : (own + 1) * group]
        fac_rows = lax.broadcasted_iota(jnp.int32, factor.shape, 0)
        fac_cols = lax.broadcasted_iota(jnp.int32, factor.shape, 1)
        own_row = jnp.logical_and(fac_rows >= start, fac_rows < start + STEP)
        own_col = jnp.logical_and(fac_cols >= offset, fac_cols < offset + STEP)
        work_ref[:, own * group : (own + 1) * group] = jnp.where(own_col, 0.0, factor)
        factor = jnp.where(jnp.logical_and(own_col, jnp.logical_not(own_row)), factor, 0.0)
        whole = jnp.concatenate(block, axis=1)
        if group >= 4 * STEP:
            high, low = split(factor)
            factor = high + pltpu.roll(high, STEP, 1) + pltpu.roll(low, 2 * STEP, 1)
            whole_high, whole_low = (part.astype(BF16) for part in split(whole))
            pieces = [jnp.zeros((STEP, tile), BF16) for _ in range(group // STEP)]
            place = offset // STEP
            for shift, part in enumerate((whole_high, whole_low, whole_high)):
                pieces[(place + shift) % len(pieces)] = part
            update = jnp.dot(
                factor.astype(BF16), jnp.concatenate(pieces, axis=0), preferred_element_type=F32
            )
        else:
            update = jnp.dot(
                factor[:, offset : offset + STEP], whole, precision=HIGHEST, preferred_element_type=F32
            )
        work_ref[...] = work_ref[...] - update
        work_ref[rows, :] = whole


def solve_kernel(front_of, place_of, meta_ref, diag_ref, gathered_ref, out_ref, work_ref, chosen_ref):
    tile = out_ref.shape[0]
    count, length = gathered_ref.shape[0], gathered_ref.shape[2]
    place = place_of(meta_ref)
    for piece in range(count):
        rows = pl.ds(pl.multiple_of((place ^ piece) * length, length), length)
        work_ref[rows, :] = gathered_ref[piece, 0].astype(F32)
        chosen_ref[rows, :] = gathered_ref[piece, 1].astype(F32)
    pivot = work_ref[...]
    rows = lax.broadcasted_iota(jnp.int32, (tile, tile), 0)
    columns = lax.broadcasted_iota(jnp.int32, (tile, tile), 1)
    diagonal = diag_ref[pl.ds(front_of(meta_ref[0]), 1), :]
    work_ref[...] = (pivot + pivot.T) * 0.5 + jnp.where(rows == columns, diagonal, 0.0)
    invert(work_ref)
    out_ref[...] = dot3(work_ref[...], chosen_ref[...], ((1,), (1,))).astype(BF16)


def lower_front(level):
    return level // 2


def upper_front(level):
    return 4 + level // 4


def pair_place(meta_ref):
    return (meta_ref[0] & 1) * 4 + (meta_ref[1] >> 1)


def no_place(meta_ref):
    return jnp.int32(0)


def solve(front_of, place_of, meta, diagonals, gathered):
    tile = gathered.shape[-1]
    return call(
        functools.partial(solve_kernel, front_of, place_of),
        jax.ShapeDtypeStruct((tile, tile), BF16),
        [SMEM, VMEM, VMEM],
        VMEM,
        [pltpu.VMEM((tile, tile), F32), pltpu.VMEM((tile, tile), F32)],
        flops=2**29,
        moved=2**22,
    )(meta, diagonals, gathered)


def pivot_slot_of(slots_ref, front):
    slot = jnp.int32(0)
    for index in range(8):
        slot = jnp.where(slots_ref[front, index] == 0, index, slot)
    return slot


def lower_kernel(
    meta_ref, slots_ref, place_ref, chunks_ref, pivot_ref, solved_ref, keep_ref, send_ref, spread_ref, stay_ref, total_ref, update_ref
):
    level, row, col = meta_ref[0], meta_ref[1], meta_ref[2]
    total_ref[...] = jnp.zeros_like(total_ref)
    half = chunks_ref.shape[0] // 2
    for child in range(2):
        dropped = pivot_slot_of(slots_ref, level // 4 * 2 + child) == col
        pivot = pivot_ref[child * half : (child + 1) * half]
        update = jnp.dot(
            pivot.reshape(-1, pivot.shape[-1]), solved_ref[child], preferred_element_type=F32
        )
        update_ref[...] = update.reshape(update_ref.shape)

        def one(index, carry):
            place = jnp.where(dropped, 128, place_ref[child * half + index])
            value = chunks_ref[child * half + index].astype(F32) - update_ref[index]
            total_ref[place] = total_ref[place] + value
            return carry

        lax.fori_loop(0, half, one, 0, unroll=4)
    keep_ref[...] = total_ref[:64]
    send_ref[...] = total_ref[64:128].astype(BF16)
    first = row % 2 * 64
    length, tile = total_ref.shape[1], total_ref.shape[2]
    for column in range(8):
        for part, ref in enumerate((stay_ref, spread_ref)):
            value = total_ref[part * 64 + column * 8 : part * 64 + column * 8 + 8]
            ref[column, : 8 * length] = value.astype(BF16).reshape(8 * length, tile)
        panel_tile = first + 8 * slots_ref[4 + level // 4, column]
        spread_ref[column, 8 * length : 9 * length] = total_ref[first].astype(BF16)
        spread_ref[column, 9 * length : 10 * length] = total_ref[panel_tile].astype(BF16)


def upper_kernel(meta_ref, slots_ref, keep_ref, sent_ref, pivot_ref, solved_ref, out_ref):
    level, row, col = meta_ref[0], meta_ref[1], meta_ref[2]
    tile = keep_ref.shape[1]
    dropped = pivot_slot_of(slots_ref, 4 + level // 4) == col
    update = jnp.dot(pivot_ref[...], solved_ref[...], preferred_element_type=F32)
    front = keep_ref[...] + sent_ref[...].astype(F32)
    result = jnp.where(dropped, 0.0, front - update)
    top = jnp.logical_and(
        lax.broadcasted_iota(jnp.int32, result.shape, 0) < tile // 16, row % 2 == 0
    )
    result = jnp.where(top, 0.0, result).astype(BF16)
    out_ref[...] = result.reshape(out_ref.shape)


def lane_groups(levels):
    groups = []
    for first in range(0, 8, levels):
        for half in range(2):
            groups.append(
                [
                    (first + level) * 8 + 2 * across + half
                    for level in range(levels)
                    for across in range(4)
                ]
            )
    return groups


def exchange(value, levels):
    return lax.all_to_all(
        value,
        ("level", "row"),
        split_axis=0,
        concat_axis=0,
        axis_index_groups=lane_groups(levels),
        tiled=True,
    )


def over_columns(value):
    return lax.all_to_all(value, "col", split_axis=0, concat_axis=0, tiled=True)


def swapped(value, axis, mask):
    return lax.ppermute(value, axis, [(index, index ^ mask) for index in range(8)])


def tied(*values):
    return lax.optimization_barrier(values)


def picked(pieces, slot):
    return lax.dynamic_index_in_dim(pieces, slot, 0, keepdims=False)


def repeated(value, count):
    return jnp.broadcast_to(value[None], (count,) + value.shape)


def body(leaf_blocks, leaf_tiles, leaf_maps, upper_maps, front_slots, pivot_diag):
    tile = leaf_blocks.shape[2]
    level = lax.axis_index("level")
    row = lax.axis_index("row")
    col = lax.axis_index("col")
    meta = jnp.stack([level, row, col]).astype(jnp.int32)
    positions = jnp.arange(8, dtype=jnp.int32)
    slots = jnp.sum(jnp.where(front_slots == 0, positions[None, :], 0), axis=1)
    eighth, sixteenth = tile // 8, tile // 16
    own = leaf_blocks.reshape(12, tile, tile)

    shares = call(
        share_kernel,
        jax.ShapeDtypeStruct((8, 8, eighth, tile), BF16),
        [SMEM] * 3 + [VMEM],
        VMEM,
        moved=2**21,
    )(meta, leaf_tiles, leaf_maps, own)
    shares = exchange(shares, 2)
    chunks = jnp.swapaxes(own.reshape(12, 16, sixteenth, tile), 0, 1)
    chunks, shares = tied(chunks, shares)
    chunks = exchange(chunks, 4).reshape(8, -1, tile)
    place = call(
        plan_kernel,
        jax.ShapeDtypeStruct((192,), jnp.int32),
        [SMEM] * 4,
        SMEM,
    )(meta, leaf_tiles, leaf_maps, upper_maps)

    shares = call(
        combine_kernel,
        jax.ShapeDtypeStruct((8, eighth, tile), BF16),
        [VMEM],
        VMEM,
        moved=2**21,
    )(shares)
    away = col ^ picked(slots, level // 2)
    for mask in (1, 2, 4):
        shares = jnp.where(away & mask == 0, shares, swapped(shares, "col", mask))
    my_tile = lax.dynamic_slice(front_slots, (level // 2, col), (1, 1))[0, 0]
    parts = jnp.stack([shares[0], picked(shares, my_tile)])
    parts = (parts.astype(F32) + swapped(parts, "row", 1).astype(F32)).astype(BF16)

    chunks, parts = tied(chunks, parts)
    pieces = over_columns(chunks)
    gathered = parts[None]
    for axis, mask in (("row", 2), ("row", 4), ("level", 1)):
        gathered = jnp.concatenate([gathered, swapped(gathered, axis, mask)], axis=0)
    piece = picked(pieces, picked(slots, level // 4 * 2 + col // 4))
    piece, gathered = tied(piece, gathered)
    pivot_columns = over_columns(repeated(piece, 8)).reshape(192, sixteenth, tile)
    solved = solve(lower_front, pair_place, meta, pivot_diag, gathered)
    other = swapped(solved, "level", 2)
    first_child = level // 2 % 2 == 0
    solved = jnp.where(first_child, jnp.stack([solved, other]), jnp.stack([other, solved]))
    keep, send, spread, stay = call(
        lower_kernel,
        (
            jax.ShapeDtypeStruct((64, sixteenth, tile), F32),
            jax.ShapeDtypeStruct((64, sixteenth, tile), BF16),
            jax.ShapeDtypeStruct((8, 10 * sixteenth, tile), BF16),
            jax.ShapeDtypeStruct((8, 8 * sixteenth, tile), BF16),
        ),
        [SMEM, SMEM, SMEM, VMEM, VMEM, VMEM],
        None,
        [pltpu.VMEM((129, sixteenth, tile), F32), pltpu.VMEM((96, sixteenth, tile), F32)],
        flops=2**29,
        moved=2**23,
    )(meta, front_slots, place, chunks.reshape(192, sixteenth, tile), pivot_columns, solved)

    upper_slot = picked(slots, 4 + level // 4)
    spread, stay = tied(picked(over_columns(spread), upper_slot), stay)
    passed = swapped(spread, "row", 1).astype(F32)
    stay = picked(over_columns(stay), upper_slot)
    piece = (stay.astype(F32) + passed[: 8 * sixteenth]).astype(BF16)
    parts = (spread[8 * sixteenth :].astype(F32) + passed[8 * sixteenth :]).astype(BF16)
    piece, parts = tied(piece, parts)
    gathered = exchange(repeated(parts.reshape(2, sixteenth, tile), 16), 4)
    sent = swapped(send, "row", 1)
    piece, gathered = tied(piece, gathered)
    pivot_columns = over_columns(repeated(piece, 8)).reshape(-1, tile)
    solved = solve(upper_front, no_place, meta, pivot_diag, gathered)
    finished = call(
        upper_kernel,
        jax.ShapeDtypeStruct((16, 4, sixteenth, tile), BF16),
        [SMEM, SMEM, VMEM, VMEM, VMEM, VMEM],
        VMEM,
        flops=2**28,
        moved=2**22,
    )(
        meta,
        front_slots,
        keep.reshape(-1, tile),
        sent.reshape(-1, tile),
        pivot_columns,
        solved,
    )
    result = exchange(finished, 4)
    return jnp.swapaxes(result, 0, 1).reshape(1, -1, tile)


def solution(mesh):
    return jax.shard_map(
        body,
        mesh=mesh,
        in_specs=(P("level", "row", "col"), P(), P(), P(), P(), P()),
        out_specs=P("level", "row", "col"),
        check_vma=False,
    )
```

```python
import functools

import jax
import jax.numpy as jnp
from jax import lax
from jax.experimental import pallas as pl
from jax.experimental.pallas import tpu as pltpu
from jax.sharding import PartitionSpec as P

TILE = 256
NPT = 128
STEP = 32
GROUP = 128
AHEAD = 3
HIGHEST = lax.Precision.HIGHEST
VMEM = pltpu.VMEM
SMEM = pltpu.SMEM
INTERPRET = False
F32 = jnp.float32
BF16 = jnp.bfloat16


def call(kernel, out_shape, in_spaces, out_space=None, scratch=(), flops=0, moved=0):
    return pl.pallas_call(
        kernel,
        out_shape=out_shape,
        in_specs=[pl.BlockSpec(memory_space=space) for space in in_spaces],
        out_specs=pl.BlockSpec(memory_space=out_space)
        if out_space is not None
        else [pl.BlockSpec(memory_space=VMEM) for _ in out_shape],
        scratch_shapes=list(scratch),
        compiler_params=pltpu.CompilerParams(vmem_limit_bytes=32 * 2**20),
        cost_estimate=pl.CostEstimate(flops=flops, bytes_accessed=moved, transcendentals=0),
        interpret=INTERPRET,
    )


def plan_kernel(meta_ref, tiles_ref, leaf_maps_ref, upper_maps_ref, place_ref):
    half = meta_ref[1] & 1
    base = meta_ref[0] & 4
    for source in range(16):
        leaf = base + source // 4
        front = (base >> 1) + source // 8
        live = tiles_ref[leaf]
        first = (2 * (source % 4) + half) * 12
        for tile in range(12):
            lower_tile = leaf_maps_ref[leaf, first + tile]
            upper_tile = upper_maps_ref[front, lower_tile]
            home_row = (upper_tile >> 2) & 7
            position = ((upper_tile >> 5) << 4) + ((home_row >> 1) << 2) + (upper_tile & 3)
            position = position + (((home_row & 1) ^ half) << 6)
            kept = jnp.logical_and(first + tile < live, lower_tile != 0)
            place_ref[source * 12 + tile] = jnp.where(kept, position, 128)


def share_kernel(meta_ref, tiles_ref, leaf_maps_ref, leaf_ref, out_ref):
    level, row = meta_ref[0], meta_ref[1]
    tile = leaf_ref.shape[1]
    across, rows = out_ref.shape[0], out_ref.shape[2]
    out_ref[...] = jnp.zeros_like(out_ref)

    def look(index, carry):
        leaf_tile = row * 12 + index
        lower_tile = leaf_maps_ref[level, leaf_tile]
        match = jnp.logical_and(lower_tile % 16 == 0, leaf_tile < tiles_ref[level])

        @pl.when(match)
        def _():
            out_ref[:, lower_tile // 16] = leaf_ref[index].reshape(across, rows, tile)

        return carry

    lax.fori_loop(0, 12, look, 0)


def combine_kernel(shares_ref, out_ref):
    total = shares_ref[0].astype(F32)
    for source in range(1, shares_ref.shape[0]):
        total = total + shares_ref[source].astype(F32)
    out_ref[...] = total.astype(BF16)


def split(value):
    high = value.astype(BF16).astype(F32)
    return high, value - high


def dot3(left, right, dims):
    left_high, left_low = (part.astype(BF16) for part in split(left))
    right_high, right_low = (part.astype(BF16) for part in split(right))
    product = functools.partial(
        lax.dot_general, dimension_numbers=(dims, ((), ())), preferred_element_type=F32
    )
    return (product(left_low, right_high) + product(left_high, right_low)) + product(
        left_high, right_high
    )


def invert(work_ref):
    tile = work_ref.shape[0]
    group = min(GROUP, tile)
    groups = tile // group
    ids = lax.broadcasted_iota(jnp.int32, (STEP, group), 0)
    lanes = lax.broadcasted_iota(jnp.int32, (1, group), 1)
    for start in range(0, tile, STEP):
        own = start // group
        offset = start - own * group
        rows = slice(start, start + STEP)
        block = [work_ref[rows, k * group : (k + 1) * group] for k in range(groups)]

        def column(step):
            lane = offset + step
            return jnp.broadcast_to(block[own][:, lane : lane + 1], (STEP, group))

        ahead = [column(step) for step in range(AHEAD)]
        for step in range(STEP):
            if step + AHEAD < STEP:
                ahead.append(column(step + AHEAD))
            here = ahead.pop(0)
            inverse = 1.0 / here[step : step + 1]
            pivot_row = ids == step
            pivot_lane = lanes == offset + step
            for k in range(len(ahead)):
                scaled = ahead[k][step : step + 1] * inverse
                ahead[k] = jnp.where(pivot_row, scaled, ahead[k] - here * scaled)
            for k in range(groups):
                value = block[k]
                scaled = value[step : step + 1]
                if k == own:
                    scaled = jnp.where(pivot_lane, 1.0, scaled)
                    value = jnp.where(pivot_lane, 0.0, value)
                scaled = scaled * inverse
                block[k] = jnp.where(pivot_row, scaled, value - here * scaled)
        factor = work_ref[:, own * group : (own + 1) * group]
        fac_rows = lax.broadcasted_iota(jnp.int32, factor.shape, 0)
        fac_cols = lax.broadcasted_iota(jnp.int32, factor.shape, 1)
        own_row = jnp.logical_and(fac_rows >= start, fac_rows < start + STEP)
        own_col = jnp.logical_and(fac_cols >= offset, fac_cols < offset + STEP)
        work_ref[:, own * group : (own + 1) * group] = jnp.where(own_col, 0.0, factor)
        factor = jnp.where(jnp.logical_and(own_col, jnp.logical_not(own_row)), factor, 0.0)
        whole = jnp.concatenate(block, axis=1)
        if group >= 4 * STEP:
            high, low = split(factor)
            factor = high + pltpu.roll(high, STEP, 1) + pltpu.roll(low, 2 * STEP, 1)
            whole_high, whole_low = (part.astype(BF16) for part in split(whole))
            pieces = [jnp.zeros((STEP, tile), BF16) for _ in range(group // STEP)]
            place = offset // STEP
            for shift, part in enumerate((whole_high, whole_low, whole_high)):
                pieces[(place + shift) % len(pieces)] = part
            update = jnp.dot(
                factor.astype(BF16), jnp.concatenate(pieces, axis=0), preferred_element_type=F32
            )
        else:
            update = jnp.dot(
                factor[:, offset : offset + STEP], whole, precision=HIGHEST, preferred_element_type=F32
            )
        work_ref[...] = work_ref[...] - update
        work_ref[rows, :] = whole


def solve_kernel(front_of, place_of, meta_ref, diag_ref, gathered_ref, out_ref, work_ref, chosen_ref):
    tile = out_ref.shape[0]
    count, length = gathered_ref.shape[0], gathered_ref.shape[2]
    place = place_of(meta_ref)
    for piece in range(count):
        rows = pl.ds(pl.multiple_of((place ^ piece) * length, length), length)
        work_ref[rows, :] = gathered_ref[piece, 0].astype(F32)
        chosen_ref[rows, :] = gathered_ref[piece, 1].astype(F32)
    pivot = work_ref[...]
    rows = lax.broadcasted_iota(jnp.int32, (tile, tile), 0)
    columns = lax.broadcasted_iota(jnp.int32, (tile, tile), 1)
    diagonal = diag_ref[pl.ds(front_of(meta_ref[0]), 1), :]
    work_ref[...] = (pivot + pivot.T) * 0.5 + jnp.where(rows == columns, diagonal, 0.0)
    invert(work_ref)
    out_ref[...] = dot3(work_ref[...], chosen_ref[...], ((1,), (1,))).astype(BF16)


def lower_front(level):
    return level // 2


def upper_front(level):
    return 4 + level // 4


def pair_place(meta_ref):
    return (meta_ref[0] & 1) * 4 + (meta_ref[1] >> 1)


def no_place(meta_ref):
    return jnp.int32(0)


def solve(front_of, place_of, meta, diagonals, gathered):
    tile = gathered.shape[-1]
    return call(
        functools.partial(solve_kernel, front_of, place_of),
        jax.ShapeDtypeStruct((tile, tile), BF16),
        [SMEM, VMEM, VMEM],
        VMEM,
        [pltpu.VMEM((tile, tile), F32), pltpu.VMEM((tile, tile), F32)],
        flops=2**29,
        moved=2**22,
    )(meta, diagonals, gathered)


def pivot_slot_of(slots_ref, front):
    slot = jnp.int32(0)
    for index in range(8):
        slot = jnp.where(slots_ref[front, index] == 0, index, slot)
    return slot


def lower_kernel(
    meta_ref, slots_ref, place_ref, chunks_ref, pivot_ref, solved_ref, keep_ref, send_ref, spread_ref, total_ref, update_ref
):
    level, row, col = meta_ref[0], meta_ref[1], meta_ref[2]
    total_ref[...] = jnp.zeros_like(total_ref)
    half = chunks_ref.shape[0] // 2
    for child in range(2):
        dropped = pivot_slot_of(slots_ref, level // 4 * 2 + child) == col
        pivot = pivot_ref[child * half : (child + 1) * half]
        update = jnp.dot(
            pivot.reshape(-1, pivot.shape[-1]), solved_ref[child], preferred_element_type=F32
        )
        update_ref[...] = update.reshape(update_ref.shape)

        def one(index, carry):
            place = jnp.where(dropped, 128, place_ref[child * half + index])
            value = chunks_ref[child * half + index].astype(F32) - update_ref[index]
            total_ref[place] = total_ref[place] + value
            return carry

        lax.fori_loop(0, half, one, 0, unroll=4)
    keep_ref[...] = total_ref[:64]
    send_ref[...] = total_ref[64:128].astype(BF16)
    first = row % 2 * 64
    length, tile = total_ref.shape[1], total_ref.shape[2]
    for column in range(8):
        local, side = column // 2, column % 2 * (length // 2)
        for part in range(2):
            value = jnp.concatenate(
                [
                    total_ref[part * 64 + home * 4 + local, side : side + length // 2]
                    for home in range(16)
                ],
                axis=0,
            )
            spread_ref[column, part * 8 * length : (part + 1) * 8 * length] = value.astype(BF16)
        panel_tile = first + 8 * slots_ref[4 + level // 4, column]
        spread_ref[column, 16 * length : 17 * length] = total_ref[first].astype(BF16)
        spread_ref[column, 17 * length : 18 * length] = total_ref[panel_tile].astype(BF16)


def upper_kernel(meta_ref, slots_ref, front_ref, pivot_ref, solved_ref, out_ref):
    level, row, col = meta_ref[0], meta_ref[1], meta_ref[2]
    tile = solved_ref.shape[0]
    length = tile // 16
    dropped = pivot_slot_of(slots_ref, 4 + level // 4) == col
    corner = jnp.logical_and(level % 4 == 0, row == 0)
    for index in range(4):
        rows = slice(index * tile, (index + 1) * tile)
        front = front_ref[:, index * length : (index + 1) * length].reshape(tile, tile)
        update = jnp.dot(pivot_ref[rows], solved_ref[...], preferred_element_type=F32)
        gone = jnp.logical_or(dropped, corner) if index == 0 else dropped
        out_ref[rows] = jnp.where(gone, 0.0, front.astype(F32) - update).astype(BF16)


def lane_groups(levels):
    groups = []
    for first in range(0, 8, levels):
        for half in range(2):
            groups.append(
                [
                    (first + level) * 8 + 2 * across + half
                    for level in range(levels)
                    for across in range(4)
                ]
            )
    return groups


def exchange(value, levels):
    return lax.all_to_all(
        value,
        ("level", "row"),
        split_axis=0,
        concat_axis=0,
        axis_index_groups=lane_groups(levels),
        tiled=True,
    )


def over_columns(value):
    return lax.all_to_all(value, "col", split_axis=0, concat_axis=0, tiled=True)


def swapped(value, axis, mask):
    return lax.ppermute(value, axis, [(index, index ^ mask) for index in range(8)])


def tied(*values):
    return lax.optimization_barrier(values)


def picked(pieces, slot):
    return lax.dynamic_index_in_dim(pieces, slot, 0, keepdims=False)


def repeated(value, count):
    return jnp.broadcast_to(value[None], (count,) + value.shape)


def body(leaf_blocks, leaf_tiles, leaf_maps, upper_maps, front_slots, pivot_diag):
    tile = leaf_blocks.shape[2]
    level = lax.axis_index("level")
    row = lax.axis_index("row")
    col = lax.axis_index("col")
    meta = jnp.stack([level, row, col]).astype(jnp.int32)
    positions = jnp.arange(8, dtype=jnp.int32)
    slots = jnp.sum(jnp.where(front_slots == 0, positions[None, :], 0), axis=1)
    eighth, sixteenth = tile // 8, tile // 16
    own = leaf_blocks.reshape(12, tile, tile)

    shares = call(
        share_kernel,
        jax.ShapeDtypeStruct((8, 8, eighth, tile), BF16),
        [SMEM] * 3 + [VMEM],
        VMEM,
        moved=2**21,
    )(meta, leaf_tiles, leaf_maps, own)
    shares = exchange(shares, 2)
    chunks = jnp.swapaxes(own.reshape(12, 16, sixteenth, tile), 0, 1)
    chunks, shares = tied(chunks, shares)
    chunks = exchange(chunks, 4).reshape(8, -1, tile)
    place = call(
        plan_kernel,
        jax.ShapeDtypeStruct((192,), jnp.int32),
        [SMEM] * 4,
        SMEM,
    )(meta, leaf_tiles, leaf_maps, upper_maps)

    shares = call(
        combine_kernel,
        jax.ShapeDtypeStruct((8, eighth, tile), BF16),
        [VMEM],
        VMEM,
        moved=2**21,
    )(shares)
    away = col ^ picked(slots, level // 2)
    for mask in (1, 2, 4):
        shares = jnp.where(away & mask == 0, shares, swapped(shares, "col", mask))
    my_tile = lax.dynamic_slice(front_slots, (level // 2, col), (1, 1))[0, 0]
    parts = jnp.stack([shares[0], picked(shares, my_tile)])
    parts = (parts.astype(F32) + swapped(parts, "row", 1).astype(F32)).astype(BF16)

    chunks, parts = tied(chunks, parts)
    pieces = over_columns(chunks)
    gathered = parts[None]
    for axis, mask in (("row", 2), ("row", 4), ("level", 1)):
        gathered = jnp.concatenate([gathered, swapped(gathered, axis, mask)], axis=0)
    piece = picked(pieces, picked(slots, level // 4 * 2 + col // 4))
    piece, gathered = tied(piece, gathered)
    pivot_columns = over_columns(repeated(piece, 8)).reshape(192, sixteenth, tile)
    solved = solve(lower_front, pair_place, meta, pivot_diag, gathered)
    other = swapped(solved, "level", 2)
    first_child = level // 2 % 2 == 0
    solved = jnp.where(first_child, jnp.stack([solved, other]), jnp.stack([other, solved]))
    keep, send, spread = call(
        lower_kernel,
        (
            jax.ShapeDtypeStruct((64, sixteenth, tile), F32),
            jax.ShapeDtypeStruct((64, sixteenth, tile), BF16),
            jax.ShapeDtypeStruct((8, 18 * sixteenth, tile), BF16),
        ),
        [SMEM, SMEM, SMEM, VMEM, VMEM, VMEM],
        None,
        [pltpu.VMEM((129, sixteenth, tile), F32), pltpu.VMEM((96, sixteenth, tile), F32)],
        flops=2**29,
        moved=2**23,
    )(meta, front_slots, place, chunks.reshape(192, sixteenth, tile), pivot_columns, solved)

    sent = swapped(send, "row", 1)
    spread = picked(over_columns(spread), picked(slots, 4 + level // 4))
    spread, sent = tied(spread, sent)
    front = (keep + sent.astype(F32)).astype(BF16)
    front = exchange(front.reshape(16, 4 * sixteenth, tile), 4)
    spread = spread.astype(F32)
    passed = swapped(spread[8 * sixteenth :].astype(BF16), "row", 1).astype(F32)
    piece = (spread[: 8 * sixteenth] + passed[: 8 * sixteenth]).astype(BF16)
    parts = (spread[16 * sixteenth :] + passed[8 * sixteenth :]).astype(BF16)
    piece = jnp.concatenate([piece.reshape(16, -1, tile), repeated(parts, 16)], axis=1)
    piece, front = tied(piece, front)
    piece = exchange(piece, 4)
    half = sixteenth // 2
    gathered = piece[:, half:].reshape(16, 2, sixteenth, tile)
    pivot_columns = over_columns(repeated(piece[:, :half], 8)).reshape(4, 2, 16, half, tile)
    pivot_columns = jnp.swapaxes(pivot_columns, 1, 2).reshape(-1, tile)
    solved = solve(upper_front, no_place, meta, pivot_diag, gathered)
    result = call(
        upper_kernel,
        jax.ShapeDtypeStruct((4 * tile, tile), BF16),
        [SMEM, SMEM, VMEM, VMEM, VMEM],
        VMEM,
        flops=2**28,
        moved=2**22,
    )(meta, front_slots, front, pivot_columns, solved)
    return result[None]


def solution(mesh):
    return jax.shard_map(
        body,
        mesh=mesh,
        in_specs=(P("level", "row", "col"), P(), P(), P(), P(), P()),
        out_specs=P("level", "row", "col"),
        check_vma=False,
    )
```

```python
import functools

import jax
import jax.numpy as jnp
from jax import lax
from jax.experimental import pallas as pl
from jax.experimental.pallas import tpu as pltpu
from jax.sharding import PartitionSpec as P

TILE = 256
NPT = 128
STEP = 32
GROUP = 128
AHEAD = 3
HIGHEST = lax.Precision.HIGHEST
VMEM = pltpu.VMEM
SMEM = pltpu.SMEM
INTERPRET = False
F32 = jnp.float32
BF16 = jnp.bfloat16


def call(kernel, out_shape, in_spaces, out_space=None, scratch=(), flops=0, moved=0):
    return pl.pallas_call(
        kernel,
        out_shape=out_shape,
        in_specs=[pl.BlockSpec(memory_space=space) for space in in_spaces],
        out_specs=pl.BlockSpec(memory_space=out_space)
        if out_space is not None
        else [pl.BlockSpec(memory_space=VMEM) for _ in out_shape],
        scratch_shapes=list(scratch),
        compiler_params=pltpu.CompilerParams(vmem_limit_bytes=32 * 2**20),
        cost_estimate=pl.CostEstimate(flops=flops, bytes_accessed=moved, transcendentals=0),
        interpret=INTERPRET,
    )


def plan_kernel(meta_ref, tiles_ref, leaf_maps_ref, upper_maps_ref, place_ref):
    half = meta_ref[1] & 1
    base = meta_ref[0] & 4
    for source in range(16):
        leaf = base + source // 4
        front = (base >> 1) + source // 8
        live = tiles_ref[leaf]
        first = (2 * (source % 4) + half) * 12
        for tile in range(12):
            lower_tile = leaf_maps_ref[leaf, first + tile]
            upper_tile = upper_maps_ref[front, lower_tile]
            home_row = (upper_tile >> 2) & 7
            position = ((upper_tile >> 5) << 4) + ((home_row >> 1) << 2) + (upper_tile & 3)
            position = position + (((home_row & 1) ^ half) << 6)
            kept = jnp.logical_and(first + tile < live, lower_tile != 0)
            place_ref[source * 12 + tile] = jnp.where(kept, position, 128)


def share_kernel(meta_ref, tiles_ref, leaf_maps_ref, leaf_ref, out_ref):
    level, row = meta_ref[0], meta_ref[1]
    tile = leaf_ref.shape[1]
    across, rows = out_ref.shape[0], out_ref.shape[2]
    out_ref[...] = jnp.zeros_like(out_ref)

    def look(index, carry):
        leaf_tile = row * 12 + index
        lower_tile = leaf_maps_ref[level, leaf_tile]
        match = jnp.logical_and(lower_tile % 16 == 0, leaf_tile < tiles_ref[level])

        @pl.when(match)
        def _():
            out_ref[:, lower_tile // 16] = leaf_ref[index].reshape(across, rows, tile)

        return carry

    lax.fori_loop(0, 12, look, 0)


def split(value):
    high = value.astype(BF16).astype(F32)
    return high, value - high


def dot3(left, right, dims):
    left_high, left_low = (part.astype(BF16) for part in split(left))
    right_high, right_low = (part.astype(BF16) for part in split(right))
    product = functools.partial(
        lax.dot_general, dimension_numbers=(dims, ((), ())), preferred_element_type=F32
    )
    return (product(left_low, right_high) + product(left_high, right_low)) + product(
        left_high, right_high
    )


def invert(work_ref):
    tile = work_ref.shape[0]
    group = min(GROUP, tile)
    groups = tile // group
    ids = lax.broadcasted_iota(jnp.int32, (STEP, group), 0)
    lanes = lax.broadcasted_iota(jnp.int32, (1, group), 1)
    for start in range(0, tile, STEP):
        own = start // group
        offset = start - own * group
        rows = slice(start, start + STEP)
        block = [work_ref[rows, k * group : (k + 1) * group] for k in range(groups)]

        def column(step):
            lane = offset + step
            return jnp.broadcast_to(block[own][:, lane : lane + 1], (STEP, group))

        ahead = [column(step) for step in range(AHEAD)]
        for step in range(STEP):
            if step + AHEAD < STEP:
                ahead.append(column(step + AHEAD))
            here = ahead.pop(0)
            inverse = 1.0 / here[step : step + 1]
            pivot_row = ids == step
            pivot_lane = lanes == offset + step
            for k in range(len(ahead)):
                scaled = ahead[k][step : step + 1] * inverse
                ahead[k] = jnp.where(pivot_row, scaled, ahead[k] - here * scaled)
            for k in range(groups):
                value = block[k]
                scaled = value[step : step + 1]
                if k == own:
                    scaled = jnp.where(pivot_lane, 1.0, scaled)
                    value = jnp.where(pivot_lane, 0.0, value)
                scaled = scaled * inverse
                block[k] = jnp.where(pivot_row, scaled, value - here * scaled)
        factor = work_ref[:, own * group : (own + 1) * group]
        fac_rows = lax.broadcasted_iota(jnp.int32, factor.shape, 0)
        fac_cols = lax.broadcasted_iota(jnp.int32, factor.shape, 1)
        own_row = jnp.logical_and(fac_rows >= start, fac_rows < start + STEP)
        own_col = jnp.logical_and(fac_cols >= offset, fac_cols < offset + STEP)
        work_ref[:, own * group : (own + 1) * group] = jnp.where(own_col, 0.0, factor)
        factor = jnp.where(jnp.logical_and(own_col, jnp.logical_not(own_row)), factor, 0.0)
        whole = jnp.concatenate(block, axis=1)
        if group >= 4 * STEP:
            high, low = split(factor)
            factor = high + pltpu.roll(high, STEP, 1) + pltpu.roll(low, 2 * STEP, 1)
            whole_high, whole_low = (part.astype(BF16) for part in split(whole))
            pieces = [jnp.zeros((STEP, tile), BF16) for _ in range(group // STEP)]
            place = offset // STEP
            for shift, part in enumerate((whole_high, whole_low, whole_high)):
                pieces[(place + shift) % len(pieces)] = part
            update = jnp.dot(
                factor.astype(BF16), jnp.concatenate(pieces, axis=0), preferred_element_type=F32
            )
        else:
            update = jnp.dot(
                factor[:, offset : offset + STEP], whole, precision=HIGHEST, preferred_element_type=F32
            )
        work_ref[...] = work_ref[...] - update
        work_ref[rows, :] = whole


def solve_kernel(front_of, place_of, meta_ref, diag_ref, gathered_ref, out_ref, work_ref, chosen_ref):
    tile = out_ref.shape[0]
    count, length = gathered_ref.shape[0], gathered_ref.shape[2]
    for piece in range(count):
        rows = pl.ds(pl.multiple_of(place_of(meta_ref, piece) * length, length), length)
        work_ref[rows, :] = gathered_ref[piece, 0].astype(F32)
        chosen_ref[rows, :] = gathered_ref[piece, 1].astype(F32)
    pivot = work_ref[...]
    rows = lax.broadcasted_iota(jnp.int32, (tile, tile), 0)
    columns = lax.broadcasted_iota(jnp.int32, (tile, tile), 1)
    diagonal = diag_ref[pl.ds(front_of(meta_ref[0]), 1), :]
    work_ref[...] = (pivot + pivot.T) * 0.5 + jnp.where(rows == columns, diagonal, 0.0)
    invert(work_ref)
    out_ref[...] = dot3(work_ref[...], chosen_ref[...], ((1,), (1,))).astype(BF16)


def lower_front(level):
    return level // 2


def upper_front(level):
    return 4 + level // 4


def across_place(meta_ref, piece):
    return ((meta_ref[1] >> 1) - piece) & 3


def same_place(meta_ref, piece):
    return jnp.int32(piece)


def solve(front_of, place_of, meta, diagonals, gathered):
    tile = gathered.shape[-1]
    return call(
        functools.partial(solve_kernel, front_of, place_of),
        jax.ShapeDtypeStruct((tile, tile), BF16),
        [SMEM, VMEM, VMEM],
        VMEM,
        [pltpu.VMEM((tile, tile), F32), pltpu.VMEM((tile, tile), F32)],
        flops=2**29,
        moved=2**22,
    )(meta, diagonals, gathered)


def pivot_slot_of(slots_ref, front):
    slot = jnp.int32(0)
    for index in range(8):
        slot = jnp.where(slots_ref[front, index] == 0, index, slot)
    return slot


def lower_kernel(
    meta_ref, slots_ref, place_ref, chunks_ref, pivot_ref, solved_ref, keep_ref, send_ref, spread_ref, total_ref, update_ref
):
    level, row, col = meta_ref[0], meta_ref[1], meta_ref[2]
    total_ref[...] = jnp.zeros_like(total_ref)
    half = chunks_ref.shape[0] // 2
    for child in range(2):
        dropped = pivot_slot_of(slots_ref, level // 4 * 2 + child) == col
        pivot = pivot_ref[child * half : (child + 1) * half]
        update = jnp.dot(
            pivot.reshape(-1, pivot.shape[-1]), solved_ref[child], preferred_element_type=F32
        )
        update_ref[...] = update.reshape(update_ref.shape)

        def one(index, carry):
            place = jnp.where(dropped, 128, place_ref[child * half + index])
            value = chunks_ref[child * half + index].astype(F32) - update_ref[index]
            total_ref[place] = total_ref[place] + value
            return carry

        lax.fori_loop(0, half, one, 0, unroll=4)
    keep_ref[...] = total_ref[:64]
    send_ref[...] = total_ref[64:128].astype(BF16)
    first = row % 2 * 64
    length, tile = total_ref.shape[1], total_ref.shape[2]
    for column in range(8):
        local, side = column // 2, column % 2 * (length // 2)
        for part in range(2):
            value = jnp.concatenate(
                [
                    total_ref[part * 64 + home * 4 + local, side : side + length // 2]
                    for home in range(16)
                ],
                axis=0,
            )
            spread_ref[column, part * 8 * length : (part + 1) * 8 * length] = value.astype(BF16)
        panel_tile = first + 8 * slots_ref[4 + level // 4, column]
        spread_ref[column, 16 * length : 17 * length] = total_ref[first].astype(BF16)
        spread_ref[column, 17 * length : 18 * length] = total_ref[panel_tile].astype(BF16)


def upper_kernel(meta_ref, slots_ref, front_ref, pivot_ref, solved_ref, out_ref):
    level, row, col = meta_ref[0], meta_ref[1], meta_ref[2]
    tile = solved_ref.shape[0]
    length = tile // 16
    dropped = pivot_slot_of(slots_ref, 4 + level // 4) == col
    corner = jnp.logical_and(level % 4 == 0, row == 0)
    for index in range(4):
        rows = slice(index * tile, (index + 1) * tile)
        front = front_ref[:, index * length : (index + 1) * length].reshape(tile, tile)
        update = jnp.dot(pivot_ref[rows], solved_ref[...], preferred_element_type=F32)
        gone = jnp.logical_or(dropped, corner) if index == 0 else dropped
        out_ref[rows] = jnp.where(gone, 0.0, front.astype(F32) - update).astype(BF16)


def lane_groups(levels):
    groups = []
    for first in range(0, 8, levels):
        for half in range(2):
            groups.append(
                [
                    (first + level) * 8 + 2 * across + half
                    for level in range(levels)
                    for across in range(4)
                ]
            )
    return groups


def exchange(value, levels):
    return lax.all_to_all(
        value,
        ("level", "row"),
        split_axis=0,
        concat_axis=0,
        axis_index_groups=lane_groups(levels),
        tiled=True,
    )


def over_columns(value):
    return lax.all_to_all(value, "col", split_axis=0, concat_axis=0, tiled=True)


def swapped(value, axis, mask):
    return lax.ppermute(value, axis, [(index, index ^ mask) for index in range(8)])


def turned(value, axis, step):
    pairs = [(index, ((index >> 1) + step) % 4 * 2 + (index & 1)) for index in range(8)]
    return lax.ppermute(value, axis, pairs)


def tied(*values):
    return lax.optimization_barrier(values)


def picked(pieces, slot):
    return lax.dynamic_index_in_dim(pieces, slot, 0, keepdims=False)


def repeated(value, count):
    return jnp.broadcast_to(value[None], (count,) + value.shape)


def body(leaf_blocks, leaf_tiles, leaf_maps, upper_maps, front_slots, pivot_diag):
    tile = leaf_blocks.shape[2]
    level = lax.axis_index("level")
    row = lax.axis_index("row")
    col = lax.axis_index("col")
    meta = jnp.stack([level, row, col]).astype(jnp.int32)
    positions = jnp.arange(8, dtype=jnp.int32)
    slots = jnp.sum(jnp.where(front_slots == 0, positions[None, :], 0), axis=1)
    eighth, sixteenth = tile // 8, tile // 16
    own = leaf_blocks.reshape(12, tile, tile)

    quarter = tile // 4
    shares = call(
        share_kernel,
        jax.ShapeDtypeStruct((4, 8, quarter, tile), BF16),
        [SMEM] * 3 + [VMEM],
        VMEM,
        moved=2**21,
    )(meta, leaf_tiles, leaf_maps, own)
    chunks = jnp.swapaxes(own.reshape(12, 16, sixteenth, tile), 0, 1)
    chunks = exchange(chunks, 4).reshape(8, -1, tile)
    place = call(
        plan_kernel,
        jax.ShapeDtypeStruct((192,), jnp.int32),
        [SMEM] * 4,
        SMEM,
    )(meta, leaf_tiles, leaf_maps, upper_maps)

    across = row // 2
    arrived = [turned(picked(shares, (across + step) % 4), "row", step) for step in (1, 2, 3)]
    shares = picked(shares, across)
    for value in arrived:
        shares = shares + value
    pivot_slot = picked(slots, level // 2)
    shares = jnp.where((col ^ pivot_slot) & 1 == 0, shares, swapped(shares, "col", 1))
    away = (col // 2 - pivot_slot // 2) % 4
    arrived = [turned(shares, "col", step) for step in (1, 2, 3)]
    for step, value in enumerate(arrived):
        shares = jnp.where(away == step + 1, value, shares)
    my_tile = lax.dynamic_slice(front_slots, (level // 2, col), (1, 1))[0, 0]
    parts = jnp.stack([shares[0], picked(shares, my_tile)])
    chunks, parts = tied(chunks, parts)
    pieces = over_columns(chunks)
    parts = (parts.astype(F32) + swapped(parts, "row", 1).astype(F32)).astype(BF16)
    parts = (parts.astype(F32) + swapped(parts, "level", 1).astype(F32)).astype(BF16)
    gathered = jnp.stack([parts] + [turned(parts, "row", step) for step in (1, 2, 3)])
    piece = picked(pieces, picked(slots, level // 4 * 2 + col // 4))
    piece, gathered = tied(piece, gathered)
    pivot_columns = over_columns(repeated(piece, 8)).reshape(192, sixteenth, tile)
    solved = solve(lower_front, across_place, meta, pivot_diag, gathered)
    other = swapped(solved, "level", 2)
    first_child = level // 2 % 2 == 0
    solved = jnp.where(first_child, jnp.stack([solved, other]), jnp.stack([other, solved]))
    keep, send, spread = call(
        lower_kernel,
        (
            jax.ShapeDtypeStruct((64, sixteenth, tile), F32),
            jax.ShapeDtypeStruct((64, sixteenth, tile), BF16),
            jax.ShapeDtypeStruct((8, 18 * sixteenth, tile), BF16),
        ),
        [SMEM, SMEM, SMEM, VMEM, VMEM, VMEM],
        None,
        [pltpu.VMEM((129, sixteenth, tile), F32), pltpu.VMEM((96, sixteenth, tile), F32)],
        flops=2**29,
        moved=2**23,
    )(meta, front_slots, place, chunks.reshape(192, sixteenth, tile), pivot_columns, solved)

    sent = swapped(send, "row", 1)
    spread = picked(over_columns(spread), picked(slots, 4 + level // 4))
    spread, sent = tied(spread, sent)
    front = (keep + sent.astype(F32)).astype(BF16)
    front = exchange(front.reshape(16, 4 * sixteenth, tile), 4)
    spread = spread.astype(F32)
    passed = swapped(spread[8 * sixteenth :].astype(BF16), "row", 1).astype(F32)
    piece = (spread[: 8 * sixteenth] + passed[: 8 * sixteenth]).astype(BF16)
    parts = (spread[16 * sixteenth :] + passed[8 * sixteenth :]).astype(BF16)
    piece = jnp.concatenate([piece.reshape(16, -1, tile), repeated(parts, 16)], axis=1)
    piece, front = tied(piece, front)
    piece = exchange(piece, 4)
    half = sixteenth // 2
    gathered = piece[:, half:].reshape(16, 2, sixteenth, tile)
    pivot_columns = over_columns(repeated(piece[:, :half], 8)).reshape(4, 2, 16, half, tile)
    pivot_columns = jnp.swapaxes(pivot_columns, 1, 2).reshape(-1, tile)
    solved = solve(upper_front, same_place, meta, pivot_diag, gathered)
    result = call(
        upper_kernel,
        jax.ShapeDtypeStruct((4 * tile, tile), BF16),
        [SMEM, SMEM, VMEM, VMEM, VMEM],
        VMEM,
        flops=2**28,
        moved=2**22,
    )(meta, front_slots, front, pivot_columns, solved)
    return result[None]


def solution(mesh):
    return jax.shard_map(
        body,
        mesh=mesh,
        in_specs=(P("level", "row", "col"), P(), P(), P(), P(), P()),
        out_specs=P("level", "row", "col"),
        check_vma=False,
    )
```

```python
import functools

import jax
import jax.numpy as jnp
from jax import lax
from jax.experimental import pallas as pl
from jax.experimental.pallas import tpu as pltpu
from jax.sharding import PartitionSpec as P

TILE = 256
NPT = 128
STEP = 32
GROUP = 128
AHEAD = 3
HIGHEST = lax.Precision.HIGHEST
VMEM = pltpu.VMEM
SMEM = pltpu.SMEM
INTERPRET = False
F32 = jnp.float32
BF16 = jnp.bfloat16


def call(kernel, out_shape, in_spaces, out_space=None, scratch=(), flops=0, moved=0):
    return pl.pallas_call(
        kernel,
        out_shape=out_shape,
        in_specs=[pl.BlockSpec(memory_space=space) for space in in_spaces],
        out_specs=pl.BlockSpec(memory_space=out_space)
        if out_space is not None
        else [pl.BlockSpec(memory_space=VMEM) for _ in out_shape],
        scratch_shapes=list(scratch),
        compiler_params=pltpu.CompilerParams(vmem_limit_bytes=32 * 2**20),
        cost_estimate=pl.CostEstimate(flops=flops, bytes_accessed=moved, transcendentals=0),
        interpret=INTERPRET,
    )


def plan_kernel(meta_ref, tiles_ref, leaf_maps_ref, upper_maps_ref, place_ref):
    half = meta_ref[1] & 1
    base = meta_ref[0] & 4
    for source in range(16):
        leaf = base + source // 4
        front = (base >> 1) + source // 8
        live = tiles_ref[leaf]
        first = (2 * (source % 4) + half) * 12
        for tile in range(12):
            lower_tile = leaf_maps_ref[leaf, first + tile]
            upper_tile = upper_maps_ref[front, lower_tile]
            home_row = (upper_tile >> 2) & 7
            position = ((upper_tile >> 5) << 4) + ((home_row >> 1) << 2) + (upper_tile & 3)
            position = position + (((home_row & 1) ^ half) << 6)
            kept = jnp.logical_and(first + tile < live, lower_tile != 0)
            place_ref[source * 12 + tile] = jnp.where(kept, position, 128)


def share_kernel(meta_ref, tiles_ref, leaf_maps_ref, leaf_ref, out_ref):
    level, row = meta_ref[0], meta_ref[1]
    tile = leaf_ref.shape[1]
    across, rows = out_ref.shape[0], out_ref.shape[2]
    out_ref[...] = jnp.zeros_like(out_ref)

    def look(index, carry):
        leaf_tile = row * 12 + index
        lower_tile = leaf_maps_ref[level, leaf_tile]
        match = jnp.logical_and(lower_tile % 16 == 0, leaf_tile < tiles_ref[level])

        @pl.when(match)
        def _():
            out_ref[:, lower_tile // 16] = leaf_ref[index].reshape(across, rows, tile)

        return carry

    lax.fori_loop(0, 12, look, 0)


def combine_kernel(shares_ref, out_ref):
    total = shares_ref[0].astype(F32)
    for source in range(1, shares_ref.shape[0]):
        total = total + shares_ref[source].astype(F32)
    out_ref[...] = total.astype(BF16)


def split(value):
    high = value.astype(BF16).astype(F32)
    return high, value - high


def dot3(left, right, dims):
    left_high, left_low = (part.astype(BF16) for part in split(left))
    right_high, right_low = (part.astype(BF16) for part in split(right))
    product = functools.partial(
        lax.dot_general, dimension_numbers=(dims, ((), ())), preferred_element_type=F32
    )
    return (product(left_low, right_high) + product(left_high, right_low)) + product(
        left_high, right_high
    )


def invert(work_ref):
    tile = work_ref.shape[0]
    group = min(GROUP, tile)
    groups = tile // group
    ids = lax.broadcasted_iota(jnp.int32, (STEP, group), 0)
    lanes = lax.broadcasted_iota(jnp.int32, (1, group), 1)
    for start in range(0, tile, STEP):
        own = start // group
        offset = start - own * group
        rows = slice(start, start + STEP)
        block = [work_ref[rows, k * group : (k + 1) * group] for k in range(groups)]

        def column(step):
            lane = offset + step
            return jnp.broadcast_to(block[own][:, lane : lane + 1], (STEP, group))

        ahead = [column(step) for step in range(AHEAD)]
        for step in range(STEP):
            if step + AHEAD < STEP:
                ahead.append(column(step + AHEAD))
            here = ahead.pop(0)
            inverse = 1.0 / here[step : step + 1]
            pivot_row = ids == step
            pivot_lane = lanes == offset + step
            for k in range(len(ahead)):
                scaled = ahead[k][step : step + 1] * inverse
                ahead[k] = jnp.where(pivot_row, scaled, ahead[k] - here * scaled)
            for k in range(groups):
                value = block[k]
                scaled = value[step : step + 1]
                if k == own:
                    scaled = jnp.where(pivot_lane, 1.0, scaled)
                    value = jnp.where(pivot_lane, 0.0, value)
                scaled = scaled * inverse
                block[k] = jnp.where(pivot_row, scaled, value - here * scaled)
        factor = work_ref[:, own * group : (own + 1) * group]
        fac_rows = lax.broadcasted_iota(jnp.int32, factor.shape, 0)
        fac_cols = lax.broadcasted_iota(jnp.int32, factor.shape, 1)
        own_row = jnp.logical_and(fac_rows >= start, fac_rows < start + STEP)
        own_col = jnp.logical_and(fac_cols >= offset, fac_cols < offset + STEP)
        work_ref[:, own * group : (own + 1) * group] = jnp.where(own_col, 0.0, factor)
        factor = jnp.where(jnp.logical_and(own_col, jnp.logical_not(own_row)), factor, 0.0)
        whole = jnp.concatenate(block, axis=1)
        if group >= 4 * STEP:
            high, low = split(factor)
            factor = high + pltpu.roll(high, STEP, 1) + pltpu.roll(low, 2 * STEP, 1)
            whole_high, whole_low = (part.astype(BF16) for part in split(whole))
            pieces = [jnp.zeros((STEP, tile), BF16) for _ in range(group // STEP)]
            place = offset // STEP
            for shift, part in enumerate((whole_high, whole_low, whole_high)):
                pieces[(place + shift) % len(pieces)] = part
            update = jnp.dot(
                factor.astype(BF16), jnp.concatenate(pieces, axis=0), preferred_element_type=F32
            )
        else:
            update = jnp.dot(
                factor[:, offset : offset + STEP], whole, precision=HIGHEST, preferred_element_type=F32
            )
        work_ref[...] = work_ref[...] - update
        work_ref[rows, :] = whole


def solve_kernel(front_of, place_of, meta_ref, diag_ref, gathered_ref, out_ref, work_ref, chosen_ref):
    tile = out_ref.shape[0]
    count, length = gathered_ref.shape[0], gathered_ref.shape[2]
    place = place_of(meta_ref)
    for piece in range(count):
        rows = pl.ds(pl.multiple_of((place ^ piece) * length, length), length)
        work_ref[rows, :] = gathered_ref[piece, 0].astype(F32)
        chosen_ref[rows, :] = gathered_ref[piece, 1].astype(F32)
    pivot = work_ref[...]
    rows = lax.broadcasted_iota(jnp.int32, (tile, tile), 0)
    columns = lax.broadcasted_iota(jnp.int32, (tile, tile), 1)
    diagonal = diag_ref[pl.ds(front_of(meta_ref[0]), 1), :]
    work_ref[...] = (pivot + pivot.T) * 0.5 + jnp.where(rows == columns, diagonal, 0.0)
    invert(work_ref)
    out_ref[...] = dot3(work_ref[...], chosen_ref[...], ((1,), (1,))).astype(BF16)


def lower_front(level):
    return level // 2


def upper_front(level):
    return 4 + level // 4


def pair_place(meta_ref):
    return (meta_ref[0] & 1) * 4 + (meta_ref[1] >> 1)


def no_place(meta_ref):
    return jnp.int32(0)


def solve(front_of, place_of, meta, diagonals, gathered):
    tile = gathered.shape[-1]
    return call(
        functools.partial(solve_kernel, front_of, place_of),
        jax.ShapeDtypeStruct((tile, tile), BF16),
        [SMEM, VMEM, VMEM],
        VMEM,
        [pltpu.VMEM((tile, tile), F32), pltpu.VMEM((tile, tile), F32)],
        flops=2**29,
        moved=2**22,
    )(meta, diagonals, gathered)


def pivot_slot_of(slots_ref, front):
    slot = jnp.int32(0)
    for index in range(8):
        slot = jnp.where(slots_ref[front, index] == 0, index, slot)
    return slot


def lower_kernel(
    meta_ref, slots_ref, place_ref, chunks_ref, pivot_ref, solved_ref, keep_ref, send_ref, spread_ref, total_ref, update_ref
):
    level, row, col = meta_ref[0], meta_ref[1], meta_ref[2]
    total_ref[...] = jnp.zeros_like(total_ref)
    half = chunks_ref.shape[0] // 2
    for child in range(2):
        dropped = pivot_slot_of(slots_ref, level // 4 * 2 + child) == col
        pivot = pivot_ref[child * half : (child + 1) * half]
        update = jnp.dot(
            pivot.reshape(-1, pivot.shape[-1]), solved_ref[child], preferred_element_type=F32
        )
        update_ref[...] = update.reshape(update_ref.shape)

        def one(index, carry):
            place = jnp.where(dropped, 128, place_ref[child * half + index])
            value = chunks_ref[child * half + index].astype(F32) - update_ref[index]
            total_ref[place] = total_ref[place] + value
            return carry

        lax.fori_loop(0, half, one, 0, unroll=8)
    keep_ref[...] = total_ref[:64]
    send_ref[...] = total_ref[64:128].astype(BF16)
    first = row % 2 * 64
    length, tile = total_ref.shape[1], total_ref.shape[2]
    for column in range(8):
        local, side = column // 2, column % 2 * (length // 2)
        for part in range(2):
            value = jnp.concatenate(
                [
                    total_ref[part * 64 + home * 4 + local, side : side + length // 2]
                    for home in range(16)
                ],
                axis=0,
            )
            spread_ref[column, part * 8 * length : (part + 1) * 8 * length] = value.astype(BF16)
        panel_tile = first + 8 * slots_ref[4 + level // 4, column]
        spread_ref[column, 16 * length : 17 * length] = total_ref[first].astype(BF16)
        spread_ref[column, 17 * length : 18 * length] = total_ref[panel_tile].astype(BF16)


def upper_kernel(meta_ref, slots_ref, front_ref, pivot_ref, solved_ref, out_ref):
    level, row, col = meta_ref[0], meta_ref[1], meta_ref[2]
    tile = solved_ref.shape[0]
    length = tile // 16
    dropped = pivot_slot_of(slots_ref, 4 + level // 4) == col
    corner = jnp.logical_and(level % 4 == 0, row == 0)
    for index in range(4):
        rows = slice(index * tile, (index + 1) * tile)
        front = front_ref[:, index * length : (index + 1) * length].reshape(tile, tile)
        update = jnp.dot(pivot_ref[rows], solved_ref[...], preferred_element_type=F32)
        gone = jnp.logical_or(dropped, corner) if index == 0 else dropped
        out_ref[rows] = jnp.where(gone, 0.0, front.astype(F32) - update).astype(BF16)


def lane_groups(levels):
    groups = []
    for first in range(0, 8, levels):
        for half in range(2):
            groups.append(
                [
                    (first + level) * 8 + 2 * across + half
                    for level in range(levels)
                    for across in range(4)
                ]
            )
    return groups


def exchange(value, levels):
    return lax.all_to_all(
        value,
        ("level", "row"),
        split_axis=0,
        concat_axis=0,
        axis_index_groups=lane_groups(levels),
        tiled=True,
    )


def over_columns(value):
    return lax.all_to_all(value, "col", split_axis=0, concat_axis=0, tiled=True)


def swapped(value, axis, mask):
    return lax.ppermute(value, axis, [(index, index ^ mask) for index in range(8)])


def tied(*values):
    return lax.optimization_barrier(values)


def picked(pieces, slot):
    return lax.dynamic_index_in_dim(pieces, slot, 0, keepdims=False)


def repeated(value, count):
    return jnp.broadcast_to(value[None], (count,) + value.shape)


def body(leaf_blocks, leaf_tiles, leaf_maps, upper_maps, front_slots, pivot_diag):
    tile = leaf_blocks.shape[2]
    level = lax.axis_index("level")
    row = lax.axis_index("row")
    col = lax.axis_index("col")
    meta = jnp.stack([level, row, col]).astype(jnp.int32)
    positions = jnp.arange(8, dtype=jnp.int32)
    slots = jnp.sum(jnp.where(front_slots == 0, positions[None, :], 0), axis=1)
    eighth, sixteenth = tile // 8, tile // 16
    own = leaf_blocks.reshape(12, tile, tile)

    shares = call(
        share_kernel,
        jax.ShapeDtypeStruct((8, 8, eighth, tile), BF16),
        [SMEM] * 3 + [VMEM],
        VMEM,
        moved=2**21,
    )(meta, leaf_tiles, leaf_maps, own)
    shares = exchange(shares, 2)
    chunks = jnp.swapaxes(own.reshape(12, 16, sixteenth, tile), 0, 1)
    chunks, shares = tied(chunks, shares)
    chunks = exchange(chunks, 4).reshape(8, -1, tile)
    place = call(
        plan_kernel,
        jax.ShapeDtypeStruct((192,), jnp.int32),
        [SMEM] * 4,
        SMEM,
    )(meta, leaf_tiles, leaf_maps, upper_maps)

    shares = call(
        combine_kernel,
        jax.ShapeDtypeStruct((8, eighth, tile), BF16),
        [VMEM],
        VMEM,
        moved=2**21,
    )(shares)
    away = col ^ picked(slots, level // 2)
    for mask in (1, 2, 4):
        shares = jnp.where(away & mask == 0, shares, swapped(shares, "col", mask))
    my_tile = lax.dynamic_slice(front_slots, (level // 2, col), (1, 1))[0, 0]
    parts = jnp.stack([shares[0], picked(shares, my_tile)])
    chunks, parts = tied(chunks, parts)
    pieces = over_columns(chunks)
    parts = (parts.astype(F32) + swapped(parts, "row", 1).astype(F32)).astype(BF16)
    gathered = parts[None]
    for axis, mask in (("row", 2), ("row", 4), ("level", 1)):
        gathered = jnp.concatenate([gathered, swapped(gathered, axis, mask)], axis=0)
    piece = picked(pieces, picked(slots, level // 4 * 2 + col // 4))
    piece, gathered = tied(piece, gathered)
    pivot_columns = over_columns(repeated(piece, 8)).reshape(192, sixteenth, tile)
    solved = solve(lower_front, pair_place, meta, pivot_diag, gathered)
    other = swapped(solved, "level", 2)
    first_child = level // 2 % 2 == 0
    solved = jnp.where(first_child, jnp.stack([solved, other]), jnp.stack([other, solved]))
    keep, send, spread = call(
        lower_kernel,
        (
            jax.ShapeDtypeStruct((64, sixteenth, tile), F32),
            jax.ShapeDtypeStruct((64, sixteenth, tile), BF16),
            jax.ShapeDtypeStruct((8, 18 * sixteenth, tile), BF16),
        ),
        [SMEM, SMEM, SMEM, VMEM, VMEM, VMEM],
        None,
        [pltpu.VMEM((129, sixteenth, tile), F32), pltpu.VMEM((96, sixteenth, tile), F32)],
        flops=2**29,
        moved=2**23,
    )(meta, front_slots, place, chunks.reshape(192, sixteenth, tile), pivot_columns, solved)

    sent = swapped(send, "row", 1)
    spread = picked(over_columns(spread), picked(slots, 4 + level // 4))
    spread, sent = tied(spread, sent)
    front = (keep + sent.astype(F32)).astype(BF16)
    front = exchange(front.reshape(16, 4 * sixteenth, tile), 4)
    spread = spread.astype(F32)
    passed = swapped(spread[8 * sixteenth :].astype(BF16), "row", 1).astype(F32)
    piece = (spread[: 8 * sixteenth] + passed[: 8 * sixteenth]).astype(BF16)
    parts = (spread[16 * sixteenth :] + passed[8 * sixteenth :]).astype(BF16)
    piece = jnp.concatenate([piece.reshape(16, -1, tile), repeated(parts, 16)], axis=1)
    piece, front = tied(piece, front)
    piece = exchange(piece, 4)
    half = sixteenth // 2
    gathered = piece[:, half:].reshape(16, 2, sixteenth, tile)
    pivot_columns = over_columns(repeated(piece[:, :half], 8)).reshape(4, 2, 16, half, tile)
    pivot_columns = jnp.swapaxes(pivot_columns, 1, 2).reshape(-1, tile)
    solved = solve(upper_front, no_place, meta, pivot_diag, gathered)
    result = call(
        upper_kernel,
        jax.ShapeDtypeStruct((4 * tile, tile), BF16),
        [SMEM, SMEM, VMEM, VMEM, VMEM],
        VMEM,
        flops=2**28,
        moved=2**22,
    )(meta, front_slots, front, pivot_columns, solved)
    return result[None]


def solution(mesh):
    return jax.shard_map(
        body,
        mesh=mesh,
        in_specs=(P("level", "row", "col"), P(), P(), P(), P(), P()),
        out_specs=P("level", "row", "col"),
        check_vma=False,
    )
```

```python
import functools

import jax
import jax.numpy as jnp
from jax import lax
from jax.experimental import pallas as pl
from jax.experimental.pallas import tpu as pltpu
from jax.sharding import PartitionSpec as P

TILE = 256
NPT = 128
STEP = 32
GROUP = 128
AHEAD = 3
HIGHEST = lax.Precision.HIGHEST
VMEM = pltpu.VMEM
SMEM = pltpu.SMEM
INTERPRET = False
F32 = jnp.float32
BF16 = jnp.bfloat16


def call(kernel, out_shape, in_spaces, out_space=None, scratch=(), flops=0, moved=0):
    return pl.pallas_call(
        kernel,
        out_shape=out_shape,
        in_specs=[pl.BlockSpec(memory_space=space) for space in in_spaces],
        out_specs=pl.BlockSpec(memory_space=out_space)
        if out_space is not None
        else [pl.BlockSpec(memory_space=VMEM) for _ in out_shape],
        scratch_shapes=list(scratch),
        compiler_params=pltpu.CompilerParams(vmem_limit_bytes=32 * 2**20),
        cost_estimate=pl.CostEstimate(flops=flops, bytes_accessed=moved, transcendentals=0),
        interpret=INTERPRET,
    )


def plan_kernel(meta_ref, tiles_ref, leaf_maps_ref, upper_maps_ref, place_ref):
    half = meta_ref[1] & 1
    base = meta_ref[0] & 4
    for source in range(16):
        leaf = base + source // 4
        front = (base >> 1) + source // 8
        live = tiles_ref[leaf]
        first = (2 * (source % 4) + half) * 12
        for tile in range(12):
            lower_tile = leaf_maps_ref[leaf, first + tile]
            upper_tile = upper_maps_ref[front, lower_tile]
            home_row = (upper_tile >> 2) & 7
            position = ((upper_tile >> 5) << 4) + ((home_row >> 1) << 2) + (upper_tile & 3)
            position = position + (((home_row & 1) ^ half) << 6)
            kept = jnp.logical_and(first + tile < live, lower_tile != 0)
            place_ref[source * 12 + tile] = jnp.where(kept, position, 128)


def share_kernel(meta_ref, tiles_ref, leaf_maps_ref, leaf_ref, out_ref):
    level, row = meta_ref[0], meta_ref[1]
    tile = leaf_ref.shape[1]
    across, rows = out_ref.shape[0], out_ref.shape[2]
    out_ref[...] = jnp.zeros_like(out_ref)

    def look(index, carry):
        leaf_tile = row * 12 + index
        lower_tile = leaf_maps_ref[level, leaf_tile]
        match = jnp.logical_and(lower_tile % 16 == 0, leaf_tile < tiles_ref[level])

        @pl.when(match)
        def _():
            out_ref[:, lower_tile // 16] = leaf_ref[index].reshape(across, rows, tile)

        return carry

    lax.fori_loop(0, 12, look, 0)


def combine_kernel(shares_ref, out_ref):
    total = shares_ref[0].astype(F32)
    for source in range(1, shares_ref.shape[0]):
        total = total + shares_ref[source].astype(F32)
    out_ref[...] = total.astype(BF16)


def split(value):
    high = value.astype(BF16).astype(F32)
    return high, value - high


def dot3(left, right, dims):
    left_high, left_low = (part.astype(BF16) for part in split(left))
    right_high, right_low = (part.astype(BF16) for part in split(right))
    product = functools.partial(
        lax.dot_general, dimension_numbers=(dims, ((), ())), preferred_element_type=F32
    )
    return (product(left_low, right_high) + product(left_high, right_low)) + product(
        left_high, right_high
    )


def invert(work_ref):
    tile = work_ref.shape[0]
    group = min(GROUP, tile)
    groups = tile // group
    ids = lax.broadcasted_iota(jnp.int32, (STEP, group), 0)
    lanes = lax.broadcasted_iota(jnp.int32, (1, group), 1)
    for start in range(0, tile, STEP):
        own = start // group
        offset = start - own * group
        rows = slice(start, start + STEP)
        block = [work_ref[rows, k * group : (k + 1) * group] for k in range(groups)]

        def column(step):
            lane = offset + step
            return jnp.broadcast_to(block[own][:, lane : lane + 1], (STEP, group))

        ahead = [column(step) for step in range(AHEAD)]
        for step in range(STEP):
            if step + AHEAD < STEP:
                ahead.append(column(step + AHEAD))
            here = ahead.pop(0)
            inverse = 1.0 / here[step : step + 1]
            pivot_row = ids == step
            pivot_lane = lanes == offset + step
            for k in range(len(ahead)):
                scaled = ahead[k][step : step + 1] * inverse
                ahead[k] = jnp.where(pivot_row, scaled, ahead[k] - here * scaled)
            for k in range(groups):
                value = block[k]
                scaled = value[step : step + 1]
                if k == own:
                    scaled = jnp.where(pivot_lane, 1.0, scaled)
                    value = jnp.where(pivot_lane, 0.0, value)
                scaled = scaled * inverse
                block[k] = jnp.where(pivot_row, scaled, value - here * scaled)
        factor = work_ref[:, own * group : (own + 1) * group]
        fac_rows = lax.broadcasted_iota(jnp.int32, factor.shape, 0)
        fac_cols = lax.broadcasted_iota(jnp.int32, factor.shape, 1)
        own_row = jnp.logical_and(fac_rows >= start, fac_rows < start + STEP)
        own_col = jnp.logical_and(fac_cols >= offset, fac_cols < offset + STEP)
        work_ref[:, own * group : (own + 1) * group] = jnp.where(own_col, 0.0, factor)
        factor = jnp.where(jnp.logical_and(own_col, jnp.logical_not(own_row)), factor, 0.0)
        whole = jnp.concatenate(block, axis=1)
        if group >= 4 * STEP:
            high, low = split(factor)
            factor = high + pltpu.roll(high, STEP, 1) + pltpu.roll(low, 2 * STEP, 1)
            whole_high, whole_low = (part.astype(BF16) for part in split(whole))
            pieces = [jnp.zeros((STEP, tile), BF16) for _ in range(group // STEP)]
            place = offset // STEP
            for shift, part in enumerate((whole_high, whole_low, whole_high)):
                pieces[(place + shift) % len(pieces)] = part
            update = jnp.dot(
                factor.astype(BF16), jnp.concatenate(pieces, axis=0), preferred_element_type=F32
            )
        else:
            update = jnp.dot(
                factor[:, offset : offset + STEP], whole, precision=HIGHEST, preferred_element_type=F32
            )
        work_ref[...] = work_ref[...] - update
        work_ref[rows, :] = whole


def solve_kernel(front_of, place_of, meta_ref, diag_ref, gathered_ref, out_ref, work_ref, chosen_ref):
    tile = out_ref.shape[0]
    count, length = gathered_ref.shape[0], gathered_ref.shape[2]
    place = place_of(meta_ref)
    for piece in range(count):
        rows = pl.ds(pl.multiple_of((place ^ piece) * length, length), length)
        work_ref[rows, :] = gathered_ref[piece, 0].astype(F32)
        chosen_ref[rows, :] = gathered_ref[piece, 1].astype(F32)
    pivot = work_ref[...]
    rows = lax.broadcasted_iota(jnp.int32, (tile, tile), 0)
    columns = lax.broadcasted_iota(jnp.int32, (tile, tile), 1)
    diagonal = diag_ref[pl.ds(front_of(meta_ref[0]), 1), :]
    work_ref[...] = (pivot + pivot.T) * 0.5 + jnp.where(rows == columns, diagonal, 0.0)
    invert(work_ref)
    out_ref[...] = dot3(work_ref[...], chosen_ref[...], ((1,), (1,))).astype(BF16)


def lower_front(level):
    return level // 2


def upper_front(level):
    return 4 + level // 4


def pair_place(meta_ref):
    return (meta_ref[0] & 1) * 4 + (meta_ref[1] >> 1)


def no_place(meta_ref):
    return jnp.int32(0)


def solve(front_of, place_of, meta, diagonals, gathered):
    tile = gathered.shape[-1]
    return call(
        functools.partial(solve_kernel, front_of, place_of),
        jax.ShapeDtypeStruct((tile, tile), BF16),
        [SMEM, VMEM, VMEM],
        VMEM,
        [pltpu.VMEM((tile, tile), F32), pltpu.VMEM((tile, tile), F32)],
        flops=2**29,
        moved=2**22,
    )(meta, diagonals, gathered)


def pivot_slot_of(slots_ref, front):
    slot = jnp.int32(0)
    for index in range(8):
        slot = jnp.where(slots_ref[front, index] == 0, index, slot)
    return slot


def lower_kernel(
    meta_ref, slots_ref, place_ref, chunks_ref, pivot_ref, solved_ref, keep_ref, send_ref, spread_ref, total_ref, update_ref
):
    level, row, col = meta_ref[0], meta_ref[1], meta_ref[2]
    total_ref[...] = jnp.zeros_like(total_ref)
    half = chunks_ref.shape[0] // 2
    for child in range(2):
        dropped = pivot_slot_of(slots_ref, level // 4 * 2 + child) == col
        pivot = pivot_ref[child * half : (child + 1) * half]
        update = jnp.dot(
            pivot.reshape(-1, pivot.shape[-1]), solved_ref[child], preferred_element_type=F32
        )
        update_ref[...] = update.reshape(update_ref.shape)

        def one(index, carry):
            place = jnp.where(dropped, 128, place_ref[child * half + index])
            value = chunks_ref[child * half + index].astype(F32) - update_ref[index]
            total_ref[place] = total_ref[place] + value
            return carry

        lax.fori_loop(0, half, one, 0, unroll=4)
    keep_ref[...] = total_ref[:64]
    send_ref[...] = total_ref[64:128].astype(BF16)
    first = row % 2 * 64
    length, tile = total_ref.shape[1], total_ref.shape[2]
    for column in range(8):
        local, side = column // 2, column % 2 * (length // 2)
        for part in range(2):
            value = jnp.concatenate(
                [
                    total_ref[part * 64 + home * 4 + local, side : side + length // 2]
                    for home in range(16)
                ],
                axis=0,
            )
            spread_ref[column, part * 8 * length : (part + 1) * 8 * length] = value.astype(BF16)
        panel_tile = first + 8 * slots_ref[4 + level // 4, column]
        spread_ref[column, 16 * length : 17 * length] = total_ref[first].astype(BF16)
        spread_ref[column, 17 * length : 18 * length] = total_ref[panel_tile].astype(BF16)


def upper_kernel(meta_ref, slots_ref, front_ref, pivot_ref, solved_ref, out_ref):
    level, row, col = meta_ref[0], meta_ref[1], meta_ref[2]
    tile = solved_ref.shape[0]
    length = tile // 16
    dropped = pivot_slot_of(slots_ref, 4 + level // 4) == col
    corner = jnp.logical_and(level % 4 == 0, row == 0)
    for index in range(4):
        rows = slice(index * tile, (index + 1) * tile)
        front = front_ref[:, index * length : (index + 1) * length].reshape(tile, tile)
        update = jnp.dot(pivot_ref[rows], solved_ref[...], preferred_element_type=F32)
        gone = jnp.logical_or(dropped, corner) if index == 0 else dropped
        out_ref[rows] = jnp.where(gone, 0.0, front.astype(F32) - update).astype(BF16)


def lane_groups(levels):
    groups = []
    for first in range(0, 8, levels):
        for half in range(2):
            groups.append(
                [
                    (first + level) * 8 + 2 * across + half
                    for level in range(levels)
                    for across in range(4)
                ]
            )
    return groups


def exchange(value, levels):
    return lax.all_to_all(
        value,
        ("level", "row"),
        split_axis=0,
        concat_axis=0,
        axis_index_groups=lane_groups(levels),
        tiled=True,
    )


def over_columns(value):
    return lax.all_to_all(value, "col", split_axis=0, concat_axis=0, tiled=True)


def swapped(value, axis, mask):
    return lax.ppermute(value, axis, [(index, index ^ mask) for index in range(8)])


def tied(*values):
    return lax.optimization_barrier(values)


def picked(pieces, slot):
    return lax.dynamic_index_in_dim(pieces, slot, 0, keepdims=False)


def repeated(value, count):
    return jnp.broadcast_to(value[None], (count,) + value.shape)


def body(leaf_blocks, leaf_tiles, leaf_maps, upper_maps, front_slots, pivot_diag):
    tile = leaf_blocks.shape[2]
    level = lax.axis_index("level")
    row = lax.axis_index("row")
    col = lax.axis_index("col")
    meta = jnp.stack([level, row, col]).astype(jnp.int32)
    positions = jnp.arange(8, dtype=jnp.int32)
    slots = jnp.sum(jnp.where(front_slots == 0, positions[None, :], 0), axis=1)
    eighth, sixteenth = tile // 8, tile // 16
    own = leaf_blocks.reshape(12, tile, tile)

    shares = call(
        share_kernel,
        jax.ShapeDtypeStruct((8, 8, eighth, tile), BF16),
        [SMEM] * 3 + [VMEM],
        VMEM,
        moved=2**21,
    )(meta, leaf_tiles, leaf_maps, own)
    shares = exchange(shares, 2)
    chunks = jnp.swapaxes(own.reshape(12, 16, sixteenth, tile), 0, 1)
    chunks, shares = tied(chunks, shares)
    chunks = exchange(chunks, 4).reshape(8, -1, tile)
    place = call(
        plan_kernel,
        jax.ShapeDtypeStruct((192,), jnp.int32),
        [SMEM] * 4,
        SMEM,
    )(meta, leaf_tiles, leaf_maps, upper_maps)

    shares = call(
        combine_kernel,
        jax.ShapeDtypeStruct((8, eighth, tile), BF16),
        [VMEM],
        VMEM,
        moved=2**21,
    )(shares)
    away = col ^ picked(slots, level // 2)
    for mask in (1, 2, 4):
        shares = jnp.where(away & mask == 0, shares, swapped(shares, "col", mask))
    my_tile = lax.dynamic_slice(front_slots, (level // 2, col), (1, 1))[0, 0]
    parts = jnp.stack([shares[0], picked(shares, my_tile)])
    parts = (parts.astype(F32) + swapped(parts, "row", 1).astype(F32)).astype(BF16)

    chunks, parts = tied(chunks, parts)
    pieces = over_columns(chunks)
    gathered = parts[None]
    for axis, mask in (("row", 2), ("row", 4), ("level", 1)):
        gathered = jnp.concatenate([gathered, swapped(gathered, axis, mask)], axis=0)
    piece = picked(pieces, picked(slots, level // 4 * 2 + col // 4))
    piece, gathered = tied(piece, gathered)
    pivot_columns = over_columns(repeated(piece, 8)).reshape(192, sixteenth, tile)
    solved = solve(lower_front, pair_place, meta, pivot_diag, gathered)
    other = swapped(solved, "level", 2)
    first_child = level // 2 % 2 == 0
    solved = jnp.where(first_child, jnp.stack([solved, other]), jnp.stack([other, solved]))
    keep, send, spread = call(
        lower_kernel,
        (
            jax.ShapeDtypeStruct((64, sixteenth, tile), F32),
            jax.ShapeDtypeStruct((64, sixteenth, tile), BF16),
            jax.ShapeDtypeStruct((8, 18 * sixteenth, tile), BF16),
        ),
        [SMEM, SMEM, SMEM, VMEM, VMEM, VMEM],
        None,
        [pltpu.VMEM((129, sixteenth, tile), F32), pltpu.VMEM((96, sixteenth, tile), F32)],
        flops=2**29,
        moved=2**23,
    )(meta, front_slots, place, chunks.reshape(192, sixteenth, tile), pivot_columns, solved)

    sent = swapped(send, "row", 1)
    spread = picked(over_columns(spread), picked(slots, 4 + level // 4))
    spread, sent = tied(spread, sent)
    front = (keep + sent.astype(F32)).astype(BF16)
    spread = spread.astype(F32)
    passed = swapped(spread[8 * sixteenth :].astype(BF16), "row", 1).astype(F32)
    piece = (spread[: 8 * sixteenth] + passed[: 8 * sixteenth]).astype(BF16)
    parts = (spread[16 * sixteenth :] + passed[8 * sixteenth :]).astype(BF16)
    half, whole = sixteenth // 2, 4 * sixteenth
    piece = jnp.concatenate(
        [front.reshape(16, whole, tile), repeated(parts, 16), piece.reshape(16, half, tile)], axis=1
    )
    piece = exchange(piece, 4)
    front = piece[:, :whole]
    gathered = piece[:, whole:-half].reshape(16, 2, sixteenth, tile)
    pivot_columns = over_columns(repeated(piece[:, -half:], 8)).reshape(4, 2, 16, half, tile)
    pivot_columns = jnp.swapaxes(pivot_columns, 1, 2).reshape(-1, tile)
    solved = solve(upper_front, no_place, meta, pivot_diag, gathered)
    result = call(
        upper_kernel,
        jax.ShapeDtypeStruct((4 * tile, tile), BF16),
        [SMEM, SMEM, VMEM, VMEM, VMEM],
        VMEM,
        flops=2**28,
        moved=2**22,
    )(meta, front_slots, front, pivot_columns, solved)
    return result[None]


def solution(mesh):
    return jax.shard_map(
        body,
        mesh=mesh,
        in_specs=(P("level", "row", "col"), P(), P(), P(), P(), P()),
        out_specs=P("level", "row", "col"),
        check_vma=False,
    )
```
